32 devices in a mesh: expo: 4 (over y, core), patch: 8 (over z, x).
Axes of the slice: x: 2, y: 2, z: 4, core: 2. Of those that a mesh axis runs over, the one named last changes fastest.
Arguments:
- images: bfloat16 [384, 512, 512], P(('expo', 'patch')), may hold values from -120 to 120
- block_weight: bfloat16 [384], P(('expo', 'patch')), may hold values from 0.049804688 to 0.5
- block_patch: int32 [384, 1], P(('expo', 'patch')), may hold values from 0 to 7; in each aligned block of 12 rows (0 to 11, 12 to 23, ...) at most 2 rows name the same one
- block_offset: int32 [384, 2], P(('expo', 'patch')), may hold values from 0 to 768
- kernel_index: int32 [384], P(('expo', 'patch')), may hold values from 0 to 188
- coef_table: float32 [189, 3], replicated, may hold values from 0.5 to 2
Outputs:
- coadd_map: float32 [8, 1024, 1024], P('patch', 'expo')
- weight_map: float32 [8, 1024, 1024], P('patch', 'expo')
The draws below stay inside these ranges and needn't reach their ends.
Inputs may be any that keep to these rules, and one draw needn't show every extreme that they name: `block_patch`: the 12 blocks of one device name one patch at most 2 times; in every draw some device names some patch exactly 2 times.
All inputs are finite; a program needn't handle non-finite values.
Results may differ from the reference program's by a relative error of at most 0.0043.
Values may be sent and summed in bfloat16 or wider, within the bound.
No kernel may reach another device: no remote copies, remote signals or barrier semaphores. Data moves between devices by JAX's collectives and lax.ppermute only.
A program may use at most 128 MiB of HBM per device.

```python
import math
import jax
import jax.numpy as jnp
import numpy as np
from jax import lax

BLOCK = 512
KHALF = 10
BASES = 3
CAP = 2
SIDE = 1024
MARGIN = 128
PGX = 4
CCDS = 189
BLK_DEV = 12
BLOCKS = 384
PGY = 2
N_PATCH = 8


def with_ends(values, rng, low, largest):
    extent = values.shape
    spot = [jax.random.randint(jax.random.fold_in(rng, axis), (), 0, extent[axis]) for axis in range(len(extent))]
    values = values.at[tuple(spot)].set(low)
    longest = extent.index(max(extent))
    spot[longest] = (spot[longest] + 1) % extent[longest]
    return values.at[tuple(spot)].set(largest)


def shard_levels(key, extent, split, least, top_value):
    def one(axis_at, blocks):
        draws = jax.random.uniform(jax.random.fold_in(jax.random.fold_in(key, 6), axis_at), (blocks,), jnp.float32, least / len(split), top_value / len(split))
        return jnp.repeat(jnp.exp(draws), extent[axis_at] // blocks).reshape((-1,) + (1,) * (len(extent) - axis_at - 1))

    gain = one(*split[0])
    for cut in split[1:]:
        gain = gain * one(*cut)
    return gain


def deal_out(own_key, own, number, rows, number_of, top, limit, skew):
    sequence = jax.random.permutation(own_key, number_of)
    crowded, common = load_shares(number_of, rows * top, limit, skew, True), load_shares(number_of, rows * top, limit, skew, False)
    places = jnp.arange(number_of)

    def named(tallies, rotation):
        used = int((tallies > 0).sum())
        fixed = max(1, used // 4)
        shifted = fixed + (places - fixed + rotation * (used - fixed)) % max(1, number_of - fixed)
        return jnp.zeros((number_of,), jnp.int32).at[sequence[jnp.where(places < fixed, places, shifted)]].set(jnp.asarray(tallies, jnp.int32))

    tallies = jnp.where(number % 4 == 0, named(crowded, number // 4), named(common, number - number // 4 - 1))
    mixed = jax.random.permutation(jax.random.fold_in(own, 3), number_of)
    source_of, receiver = mixed[0:number_of // 2 * 2:2], mixed[1:number_of // 2 * 2:2]
    slack = jnp.minimum(tallies[source_of] - 1, limit - tallies[receiver]) // 2
    slack = jnp.where((source_of == sequence[0]) | (receiver == sequence[0]) | (tallies[receiver] == 0), 0, jnp.maximum(slack, 0))
    shifted = jax.random.randint(jax.random.fold_in(own, 4), (number_of // 2,), 0, 1 << 20) % (slack + 1)
    tallies = tallies.at[source_of].add(-shifted).at[receiver].add(shifted)
    members = jnp.searchsorted(jnp.cumsum(tallies), jnp.arange(rows * top), side="right").astype(jnp.int32)
    listing = members.reshape(top, rows).T
    listing = listing[jax.random.permutation(jax.random.fold_in(own, 1), rows)]
    rotation = jax.random.randint(jax.random.fold_in(own, 2), (rows, 1), 0, top)
    return jnp.take_along_axis(listing, (jnp.arange(top)[None, :] + rotation) % top, axis=1)


def load_shares(amount, total, limit, slope, full):
    loads = [(1 << 20) // math.isqrt(grade ** slope) + 1 for grade in range(1, amount + 1)]
    largest = limit if full else min(limit, max(-(-total // amount), total * loads[0] // sum(loads)))
    least = 1 if total - largest >= amount - 1 else 0
    holding, rest = [largest] + [least] * (amount - 1), total - largest - least * (amount - 1)
    while rest > 0:
        candidates = [i for i in range(1, amount) if holding[i] < largest] or [i for i in range(1, amount) if holding[i] < limit]
        pool, left = sum([loads[i] for i in candidates]), rest
        for i in candidates:
            more = min(limit - holding[i], max(1, left * loads[i] // pool), rest)
            holding[i] = holding[i] + more
            rest = rest - more
    return np.array(holding)


def gaussian(rng, dims, deviation, bound, cuts=(), kind=jnp.bfloat16):
    entries = deviation * jax.random.normal(rng, dims, jnp.float32)
    if cuts:
        entries = entries * shard_levels(rng, dims, cuts, -0.22, 0.18)
    return jnp.clip(entries, -bound, bound).astype(kind)


def setup_inputs(seed: int = 0) -> dict:
    key_list = jax.random.split(jax.random.key(seed), 7)
    images = gaussian(key_list[0], (BLOCKS, BLOCK, BLOCK), 20.0, 120.0, ((0, 32),))
    block_weight = jnp.clip(jnp.exp(math.log(0.5) - 2.306499 * jax.random.uniform(key_list[1], (BLOCKS,), jnp.float32) ** shard_levels(key_list[1], (BLOCKS,), ((0, 32),), -0.2, 0.2)), 0.049804688, 0.5).astype(jnp.bfloat16)
    block_patch_keys = jax.random.split(jax.random.fold_in(key_list[2], 1), BLOCKS // BLK_DEV)
    block_patch_turns = jax.random.permutation(jax.random.fold_in(key_list[2], 3), BLOCKS // BLK_DEV)
    block_patch = jax.vmap(lambda own, number: deal_out(jax.random.fold_in(key_list[2], 2), own, number, BLK_DEV, N_PATCH, 1, CAP, 2))(block_patch_keys, block_patch_turns).reshape((BLOCKS, 1))
    block_offset = with_ends(jax.random.randint(key_list[3], (BLOCKS, 2), 0, SIDE + 2 * MARGIN - BLOCK + 1), jax.random.fold_in(key_list[3], 1), 0, SIDE + 2 * MARGIN - BLOCK).astype(jnp.int32)
    kernel_index = with_ends(jax.random.randint(key_list[4], (BLOCKS,), 0, CCDS), jax.random.fold_in(key_list[4], 1), 0, CCDS - 1).astype(jnp.int32)
    coef_table = jnp.clip(jax.random.uniform(key_list[5], (CCDS, BASES), jnp.float32, 0.5, 2.0), 0.5, 2.0)
    return dict(images=images, block_weight=block_weight, block_patch=block_patch, block_offset=block_offset, kernel_index=kernel_index, coef_table=coef_table)


SIGMAS = (0.8, 1.6, 3.2)
weight_floor = 0.5
ref_group = 16


def gauss_taps(half_width):
    offsets = jnp.arange(-half_width, half_width + 1).astype(jnp.float32)
    profiles = []
    for sigma_value in SIGMAS:
        profile = jnp.exp(-offsets * offsets / (2.0 * sigma_value * sigma_value))
        profiles.append(profile / jnp.sum(profile))
    return jnp.stack(profiles).astype(jnp.bfloat16)


def convolve_ref(pixels, coefficients, across, downward):
    planes = pixels.astype(jnp.float32)[:, None]
    spread = lax.conv_general_dilated(planes, across, (1, 1), ((0, 0), (KHALF, KHALF)), precision=lax.Precision.HIGHEST)
    scaled = (spread * coefficients[:, :, None, None]).astype(jnp.bfloat16)
    scaled = lax.optimization_barrier(scaled).astype(jnp.float32)
    merged = lax.conv_general_dilated(scaled, downward, (1, 1), ((KHALF, KHALF), (0, 0)), feature_group_count=BASES, precision=lax.Precision.HIGHEST)
    return jnp.sum(merged, axis=1).astype(jnp.bfloat16)


def reference(images, block_weight, block_patch, block_offset, kernel_index, coef_table):
    tap_count = 2 * KHALF + 1
    filter_taps = gauss_taps(KHALF).astype(jnp.float32)
    across = filter_taps.reshape(BASES, 1, 1, tap_count)
    downward = filter_taps.reshape(BASES, 1, tap_count, 1)
    groups = BLOCKS // ref_group
    span_y = PGY * SIDE + 2 * MARGIN
    span_x = PGX * SIDE + 2 * MARGIN
    canvas_start = jnp.zeros((2, span_y, span_x), jnp.float32)
    packed_all = (images.reshape(groups, ref_group, BLOCK, BLOCK), block_weight.reshape(groups, ref_group),
                  block_patch.reshape(groups, ref_group, 1), block_offset.reshape(groups, ref_group, 2),
                  kernel_index.reshape(groups, ref_group))

    def group_step(canvas, packed):
        pixels, weights, patches, corners_at, kernels = packed
        coefficients = coef_table[kernels]
        smooth = convolve_ref(pixels, coefficients, across, downward)

        def place(slot_pos, canvas_in):
            patch_id = patches[slot_pos, 0]
            row_start = (patch_id // PGX) * SIDE + corners_at[slot_pos, 0]
            col_start = (patch_id % PGX) * SIDE + corners_at[slot_pos, 1]
            plane_start = jnp.zeros((), jnp.int32)
            weight_now = weights[slot_pos].astype(jnp.float32)
            update = jnp.stack([weight_now * smooth[slot_pos].astype(jnp.float32),
                                jnp.full((BLOCK, BLOCK), weight_now, jnp.float32)])
            region = lax.dynamic_slice(canvas_in, (plane_start, row_start, col_start), (2, BLOCK, BLOCK))
            return lax.dynamic_update_slice(canvas_in, region + update, (plane_start, row_start, col_start))

        return lax.fori_loop(0, ref_group, place, canvas), None

    canvas, _ = lax.scan(group_step, canvas_start, packed_all)
    interior = canvas[:, MARGIN:MARGIN + PGY * SIDE, MARGIN:MARGIN + PGX * SIDE]
    interior = interior.reshape(2, PGY, SIDE, PGX, SIDE).transpose(0, 1, 3, 2, 4).reshape(2, N_PATCH, SIDE, SIDE)
    numerator = interior[0]
    weight_map = interior[1]
    coadd_map = numerator / jnp.maximum(weight_map, weight_floor)
    return coadd_map, weight_map
```

```python
import functools

import jax
import jax.numpy as jnp
from jax import lax
from jax.experimental import pallas as pl
from jax.experimental.pallas import tpu as pltpu
from jax.sharding import PartitionSpec as P

BLOCK = 512
KHALF = 10
BASES = 3
SIDE = 1024
MARGIN = 128
PGX = 4
SIGMAS = (0.8, 1.6, 3.2)
weight_floor = 0.5

LANES = 128
HALF = BLOCK // 2
PAD = 16
COL_PAD = BLOCK // LANES
TILE_COLS = SIDE // LANES
QUARTER_COLS = 2 * TILE_COLS
COL_TILES = QUARTER_COLS + 2 * COL_PAD
ROW_PAD = HALF + PAD


def band_rows(row_ids):
    offsets = jnp.arange(-KHALF, KHALF + 1).astype(jnp.float32)
    distance = (jnp.arange(BLOCK)[None, :] - row_ids[:, None]).astype(jnp.float32)
    rows = []
    for sigma in SIGMAS:
        total = jnp.sum(jnp.exp(-offsets * offsets / (2.0 * sigma * sigma)))
        taps = jnp.exp(-distance * distance / (2.0 * sigma * sigma)) / total
        rows.append(jnp.where(jnp.abs(distance) <= KHALF, taps, 0.0))
    return jnp.stack(rows).astype(jnp.bfloat16)


def quarter_kernel(geom, sources, has_start, split, *refs):
    stripe, slots = geom
    groups = HALF // stripe
    window = stripe + PAD
    refs = list(refs)
    where_ref = refs.pop(0)
    table_ref = refs.pop(0)
    images = [refs.pop(0) for _ in range(sources)]
    metas = [refs.pop(0) for _ in range(sources)]
    band_ref, wrap_ref = refs.pop(0), refs.pop(0)
    start_ref = refs.pop(0) if has_start else None
    outs = [refs.pop(0) for _ in range(2 if split else 1)]
    canvas, tile_buf, spread, chosen, sems = refs
    quarter, core, row_at, col_at = where_ref[0], where_ref[1], where_ref[2], where_ref[3]
    rows = slots * stripe
    inner = pl.ds(ROW_PAD, rows)

    if has_start:
        canvas[COL_PAD : COL_PAD + QUARTER_COLS, inner, :] = start_ref[...]
    else:
        canvas[COL_PAD : COL_PAD + QUARTER_COLS, inner, :] = jnp.zeros(
            (QUARTER_COLS, rows, LANES), jnp.float32
        )

    for image_ref, meta_ref in zip(images, metas):
        count_all = image_ref.shape[0]

        def corner(i, meta_ref=meta_ref):
            patch = meta_ref[i, 0].astype(jnp.int32)
            row = (patch // PGX) * SIDE + meta_ref[i, 1].astype(jnp.int32) - MARGIN
            col = (patch % PGX) * SIDE + meta_ref[i, 2].astype(jnp.int32) - MARGIN
            return row - (quarter // 2) * SIDE, col - (quarter % 2) * (2 * SIDE)

        def scan(i, count):
            row, col = corner(i)
            hit = (row > -BLOCK) & (row < SIDE) & (col > -BLOCK) & (col < 2 * SIDE)
            chosen[count] = i
            return count + hit.astype(jnp.int32)

        count = lax.fori_loop(0, count_all, scan, jnp.int32(0))

        def fetch(i, image_ref=image_ref):
            slot = lax.rem(i, 2)
            return pltpu.make_async_copy(
                image_ref.at[chosen[i]], tile_buf.at[slot], sems.at[slot]
            )

        @pl.when(count > 0)
        def _():
            fetch(0).start()

        def body(i, carry, meta_ref=meta_ref):
            @pl.when(i + 1 < count)
            def _():
                fetch(i + 1).start()

            fetch(i).wait()
            k = chosen[i]
            row, col = corner(k)
            kernel = meta_ref[k, 3].astype(jnp.int32)
            weight = meta_ref[k, 4]
            col_tile = (col + BLOCK) // LANES
            shift = col + BLOCK - col_tile * LANES
            stripe_at = (row + BLOCK) // stripe
            rho = row + BLOCK - stripe_at * stripe
            stripe_at = stripe_at - BLOCK // stripe
            parted = (stripe_at + core + 2 * BLOCK) % 2 == 0
            slot_row = jnp.where(
                parted, (stripe_at - core) // 2, (stripe_at + 1 - core) // 2
            ) * stripe
            first = jnp.where(parted, 2 * stripe - rho, stripe - rho)
            first_at = pl.multiple_of((first // PAD) * PAD, PAD)
            delta = first - first_at
            pixels = tile_buf[lax.rem(i, 2)]
            lane = lax.broadcasted_iota(jnp.int32, (window, LANES), 1)
            local = lax.broadcasted_iota(jnp.int32, (window, LANES), 0) - delta
            valid = (local >= 0) & (local < stripe)
            split_at = jnp.where(parted, rho, stripe)
            upper = valid & (local < split_at)
            lower = valid & (local >= split_at)
            for g in range(groups):
                for b in range(BASES):
                    down = jnp.dot(
                        wrap_ref[b, g, pl.ds(first_at, window), :],
                        pixels,
                        preferred_element_type=jnp.float32,
                    )
                    spread[:, b * BLOCK : (b + 1) * BLOCK] = (
                        down * table_ref[kernel, b]
                    ).astype(jnp.bfloat16)
                merged = jnp.dot(spread[...], band_ref[...], preferred_element_type=jnp.float32)
                merged = merged.astype(jnp.bfloat16).astype(jnp.float32) * weight
                turned = [
                    pltpu.roll(merged[:, j * LANES : (j + 1) * LANES], shift, 1)
                    for j in range(COL_PAD)
                ]
                base = ROW_PAD + slot_row + g * stripe - delta
                upper_at = jnp.where(parted, base + stripe, base)
                pieces = []
                for j in range(COL_PAD + 1):
                    left = turned[j - 1] if j > 0 else 0.0
                    right = turned[j] if j < COL_PAD else 0.0
                    pieces.append(jnp.where(lane < shift, left, right))
                for j, piece in enumerate(pieces):
                    at = (col_tile + j, pl.ds(upper_at, window), slice(None))
                    canvas[at] = canvas[at] + jnp.where(upper, piece, 0.0)

                @pl.when(parted)
                def _():
                    for j, piece in enumerate(pieces):
                        at = (col_tile + j, pl.ds(base, window), slice(None))
                        canvas[at] = canvas[at] + jnp.where(lower, piece, 0.0)

            return carry

        lax.fori_loop(0, count, body, 0)

    if not split:
        outs[0][...] = canvas[COL_PAD : COL_PAD + QUARTER_COLS, inner, :]
        return

    mixed = slots == 2
    for kind, out in enumerate(outs):
        for i in range(slots):
            slot = row_at ^ (slots - 1 - i)
            side = col_at if kind == 1 else 1 - col_at
            if mixed:
                odd = core == 1
                slot = jnp.where(odd, row_at ^ (1 - kind), slot)
                side = jnp.where(odd, col_at ^ (1 - i), side)
            at = pl.multiple_of(ROW_PAD + slot * stripe, PAD)
            for j in range(TILE_COLS):
                piece = canvas[COL_PAD + side * TILE_COLS + j, pl.ds(at, stripe), :]
                out[i, :, j * LANES : (j + 1) * LANES] = piece.astype(out.dtype)


def make_quarter(geom, where, table, images, metas, bands, start, split):
    stripe, slots = geom
    rows = slots * stripe
    smem = pl.BlockSpec(memory_space=pltpu.SMEM)
    vmem = pl.BlockSpec(memory_space=pltpu.VMEM)
    hbm = pl.BlockSpec(memory_space=pl.ANY)
    sources = len(images)
    has_start = start is not None
    if split:
        out_shape = [
            jax.ShapeDtypeStruct((slots, stripe, SIDE), jnp.bfloat16),
            jax.ShapeDtypeStruct((slots, stripe, SIDE), jnp.float32),
        ]
    else:
        out_shape = [jax.ShapeDtypeStruct((QUARTER_COLS, rows, LANES), jnp.float32)]
    blocks = sum(image.shape[0] for image in images) // 3
    return pl.pallas_call(
        functools.partial(quarter_kernel, geom, sources, has_start, split),
        out_shape=out_shape,
        in_specs=[smem, smem]
        + [hbm] * sources
        + [smem] * sources
        + [vmem, vmem]
        + ([vmem] if has_start else []),
        out_specs=[vmem] * len(out_shape),
        scratch_shapes=[
            pltpu.VMEM((COL_TILES, 2 * ROW_PAD + rows, LANES), jnp.float32),
            pltpu.VMEM((2, BLOCK, BLOCK), jnp.bfloat16),
            pltpu.VMEM((stripe + PAD, BASES * BLOCK), jnp.bfloat16),
            pltpu.SMEM((max(image.shape[0] for image in images) + 1,), jnp.int32),
            pltpu.SemaphoreType.DMA((2,)),
        ],
        compiler_params=pltpu.CompilerParams(vmem_limit_bytes=48 * 1024 * 1024),
        cost_estimate=pl.CostEstimate(
            flops=blocks * 4 * BASES * HALF * BLOCK * BLOCK,
            bytes_accessed=blocks * BLOCK * BLOCK * 2 + 8 * 1024 * 1024,
            transcendentals=0,
        ),
    )(where, table, *images, *metas, *bands, *([start] if has_start else []))


def on_device(
    expo_count, patch_count, images, block_weight, block_patch, block_offset, kernel_index, coef_table
):
    stripe = SIDE // expo_count
    slots = expo_count // 2
    depth = patch_count // 2
    mixed = slots == 2
    geom = (stripe, slots)
    expo, patch = lax.axis_index("expo"), lax.axis_index("patch")
    core, row_at = expo % 2, expo // 2
    col_at, layer = patch % 2, patch // 2
    everyone = [(e, p) for e in range(expo_count) for p in range(patch_count)]

    def swap(value, partner):
        route = []
        for e, p in everyone:
            to_e, to_p = partner(e, p)
            route.append((e * patch_count + p, to_e * patch_count + to_p))
        return lax.ppermute(value, ("expo", "patch"), route)

    meta = jnp.concatenate(
        [
            block_patch.astype(jnp.float32),
            block_offset.astype(jnp.float32),
            kernel_index[:, None].astype(jnp.float32),
            block_weight[:, None].astype(jnp.float32),
        ],
        axis=1,
    )
    twin_meta = swap(meta, lambda e, p: (e ^ 1, p))
    twin_images = swap(images, lambda e, p: (e ^ 1, p))

    band = band_rows(jnp.arange(BLOCK)).reshape(BASES * BLOCK, BLOCK)
    groups = HALF // stripe
    span = 3 * stripe + PAD
    wrap_ids = (
        jnp.arange(groups)[:, None] * 2 * stripe + (jnp.arange(span) % (2 * stripe))[None, :]
    ).reshape(-1)
    wrap = band_rows(wrap_ids).reshape(BASES, groups, span, BLOCK)
    bands = (band, wrap)

    def place(step):
        return jnp.stack([layer ^ step, core, row_at, col_at]).astype(jnp.int32)

    quarter = functools.partial(make_quarter, geom)
    steps = list(range(depth))[::-1]
    early = {}
    for step in steps[:2]:
        early[step] = quarter(place(step), coef_table, [images], [meta], bands, None, False)[0]

    def first_partner(e, p):
        if mixed and e % 2 == 1:
            return e ^ 2, p
        return e, p ^ 1

    arrived = []
    for step in steps:
        if step in early:
            leave, stay = quarter(
                place(step), coef_table, [twin_images], [twin_meta], bands, early[step], True
            )
        else:
            leave, stay = quarter(
                place(step), coef_table, [images, twin_images], [meta, twin_meta], bands, None, True
            )
        got = swap(leave, first_partner)
        total = stay[slots - 1] + got[slots - 1].astype(jnp.float32)
        for hop in range(1, slots):
            part = (stay[slots - 1 - hop] + got[slots - 1 - hop].astype(jnp.float32)).astype(
                jnp.bfloat16
            )

            def second_partner(e, p, hop=hop):
                if mixed and e % 2 == 1:
                    return e, p ^ 1
                return e ^ (2 * hop), p

            total = total + swap(part, second_partner).astype(jnp.float32)
        if step > 0:
            moved = swap(total.astype(jnp.bfloat16), lambda e, p, step=step: (e, p ^ (2 * step)))
            arrived.append(moved)
        else:
            arrived.append(total)

    lists = jnp.concatenate([meta, twin_meta], axis=0)
    reach = 2
    while reach < expo_count:
        lists = jnp.concatenate([lists, swap(lists, lambda e, p, r=reach: (e ^ r, p))], axis=0)
        reach *= 2
    reach = 1
    while reach < patch_count:
        lists = jnp.concatenate([lists, swap(lists, lambda e, p, r=reach: (e, p ^ r))], axis=0)
        reach *= 2
    ids = lists[:, :3].astype(jnp.int32)
    top = (ids[:, 0] // PGX) * SIDE + ids[:, 1] - MARGIN
    left = (ids[:, 0] % PGX) * SIDE + ids[:, 2] - MARGIN
    my_row = (patch // PGX) * SIDE + expo * stripe + jnp.arange(stripe)
    my_col = (patch % PGX) * SIDE + jnp.arange(SIDE)
    row_gap = my_row[:, None] - top[None, :]
    col_gap = my_col[None, :] - left[:, None]
    row_in = jnp.where((row_gap >= 0) & (row_gap < BLOCK), lists[:, 4][None, :], 0.0)
    col_in = (col_gap >= 0) & (col_gap < BLOCK)
    weight_map = jnp.dot(
        row_in.astype(jnp.bfloat16),
        col_in.astype(jnp.bfloat16),
        preferred_element_type=jnp.float32,
    )

    numerator = arrived[-1]
    for value in arrived[:-1]:
        numerator = numerator + value.astype(jnp.float32)
    coadd_map = numerator / jnp.maximum(weight_map, weight_floor)
    return (coadd_map[None], weight_map[None])


def solution(mesh):
    return jax.shard_map(
        functools.partial(on_device, mesh.shape["expo"], mesh.shape["patch"]),
        mesh=mesh,
        in_specs=(
            P(("expo", "patch"), None, None),
            P(("expo", "patch")),
            P(("expo", "patch"), None),
            P(("expo", "patch"), None),
            P(("expo", "patch")),
            P(),
        ),
        out_specs=(P("patch", "expo", None), P("patch", "expo", None)),
        check_vma=False,
    )
```

```python
import functools

import jax
import jax.numpy as jnp
import ml_dtypes
import numpy as np
from jax import lax
from jax.experimental import pallas as pl
from jax.experimental.pallas import tpu as pltpu
from jax.sharding import PartitionSpec as P

BLOCK = 512
KHALF = 10
BASES = 3
SIDE = 1024
MARGIN = 128
PGX = 4
PGX_BITS = 2
SIGMAS = (0.8, 1.6, 3.2)
weight_floor = 0.5

LANES = 128
HALF = BLOCK // 2
PAD = 16
BATCH = 4
FIELD_ROWS = 16
COL_PAD = BLOCK // LANES
TILE_COLS = SIDE // LANES
QUARTER_COLS = 2 * TILE_COLS
COL_TILES = QUARTER_COLS + 2 * COL_PAD


def taps_at(basis, distance):
    offsets = np.arange(-KHALF, KHALF + 1).astype(np.float32)
    taps = []
    for sigma in SIGMAS:
        profile = np.exp(-offsets * offsets / np.float32(2.0 * sigma * sigma))
        taps.append(profile / np.sum(profile, dtype=np.float32))
    taps = np.stack(taps).astype(ml_dtypes.bfloat16)
    inside = np.abs(distance) <= KHALF
    found = taps[basis, np.where(inside, distance + KHALF, 0)]
    return np.where(inside, found, np.zeros((), ml_dtypes.bfloat16))


def geometry(stripe):
    groups = HALF // stripe
    gap = PAD if groups == 1 else 2 * PAD
    window = stripe + PAD + gap
    parts = 2 if groups == 1 else 1
    group_rows = PAD + 2 * stripe + gap + stripe + 2 * PAD
    row_pad = HALF + PAD + gap
    return groups, gap, window, parts, group_rows, row_pad


def make_bands(stripe):
    _, _, window, parts, _, _ = geometry(stripe)
    height = window // parts
    row, col = np.indices((BASES * height, height + 2 * PAD))
    down = taps_at(row // height, col - row % height - PAD)
    row, col = np.indices((BASES * BLOCK, 6 * LANES))
    side = col // (2 * LANES)
    col = col - side * LANES
    mine = (col >= 192).astype(np.int32) + (col >= 320) == side
    across = np.where(mine, taps_at(row // BLOCK, col - row % BLOCK), 0)
    return jnp.asarray(down, jnp.bfloat16), jnp.asarray(across, jnp.bfloat16)


def quarter_kernel(geom, step, sources, has_start, split, waits, has_fields, *refs):
    stripe, slots = geom
    groups, gap, window, parts, group_rows, row_pad = geometry(stripe)
    height = window // parts
    refs = list(refs)
    table_ref, where_refs, weight_ref = refs.pop(0), [refs.pop(0) for _ in range(3)], refs.pop(0)
    patch_ref, offset_ref, index_ref = where_refs
    images = [refs.pop(0) for _ in range(sources)]
    band_hbm = [refs.pop(0), refs.pop(0)]
    start_ref = refs.pop(0) if has_start else None
    refs = refs[waits:]
    fields_ref = refs.pop(0) if has_fields else None
    outs = [refs.pop(0) for _ in range(2 if split else 1)]
    token_ref = refs.pop(0)
    canvas, tile_buf, spread, down_ref, band_ref, chosen, sems, side_sems = refs[:8]
    stages = refs[8:]
    expo, place_at = lax.axis_index("expo"), lax.axis_index("patch")
    core, row_at, col_at, quarter = expo & 1, expo >> 1, place_at & 1, (place_at >> 1) ^ step
    rows = slots * stripe
    per_source = images[0].shape[0]

    def canvas_copies(other, out):
        copies = []
        for n in range(4):
            cols = QUARTER_COLS // 4
            mine = canvas.at[pl.ds(COL_PAD + n * cols, cols), pl.ds(row_pad, rows), :]
            far = other.at[pl.ds(n * cols, cols)]
            ends = (mine, far) if out else (far, mine)
            copies.append(pltpu.make_async_copy(*ends, side_sems.at[2 + n]))
        return copies


    loads = [
        pltpu.make_async_copy(band_hbm[0], down_ref, side_sems.at[0]),
        pltpu.make_async_copy(band_hbm[1], band_ref, side_sems.at[1]),
    ]
    if has_start:
        loads += canvas_copies(start_ref, False)
    if has_fields:
        loads.append(
            pltpu.make_async_copy(
                fields_ref, outs[0].at[pl.ds(rows, FIELD_ROWS)], side_sems.at[6]
            )
        )
    token_ref[0, 0] = 0.0
    for load in loads:
        load.start()

    stripe_bits = stripe.bit_length() - 1
    row_shift = BLOCK - MARGIN - (quarter >> 1) * SIDE
    col_shift = BLOCK - MARGIN - (quarter & 1) * (2 * SIDE)

    def corner(i):
        patch = patch_ref[0, i]
        row = (patch >> PGX_BITS) * SIDE + offset_ref[0, i] + row_shift
        col = (patch & (PGX - 1)) * SIDE + offset_ref[1, i] + col_shift
        return (row >> stripe_bits) - BLOCK // stripe, row & (stripe - 1), col

    def scan(i, count):
        stripe_at, rho, col = corner(i)
        lowest = jnp.maximum(stripe_at, 0)
        lowest = lowest + ((lowest + core) & 1)
        highest = stripe_at + BLOCK // stripe - (rho == 0).astype(jnp.int32)
        hit = (lowest <= jnp.minimum(highest, 2 * slots - 1)) & (col > 0) & (col < BLOCK + 2 * SIDE)
        chosen[count] = i
        return count + hit.astype(jnp.int32)

    count = lax.fori_loop(0, sources * per_source, scan, jnp.int32(0))

    def pieces_of(g):
        top, base = 2 * stripe * g, group_rows * g
        early = PAD if g > 0 else 0
        late = PAD if g < groups - 1 else 0
        again = base + PAD + 2 * stripe + gap
        return [
            (top - early, early + 2 * stripe + late, base + PAD - early),
            (top - early, early + stripe + PAD, again - early),
        ]

    def fetch(i, slot, act):
        k = chosen[i]
        for n, image_ref in enumerate(images):

            @pl.when((k >= n * per_source) & (k < (n + 1) * per_source))
            def _():
                for g in range(groups):
                    for c, (top, size, to) in enumerate(pieces_of(g)):
                        act(
                            pltpu.make_async_copy(
                                image_ref.at[k - n * per_source, pl.ds(top, size), :],
                                tile_buf.at[slot, pl.ds(to, size), :],
                                sems.at[slot, 2 * g + c],
                            )
                        )

    def start(i, slot):
        @pl.when(i < count)
        def _():
            fetch(i, slot, lambda copy: copy.start())

    for slot in range(4):
        for g in range(groups):
            base = group_rows * g
            again = base + PAD + 2 * stripe + gap
            for top, bottom in (
                (base, base + PAD),
                (base + PAD + 2 * stripe, again),
                (again + stripe + PAD, base + group_rows),
            ):
                tile_buf[slot, top:bottom, :] = jnp.zeros((bottom - top, BLOCK), tile_buf.dtype)
    start(0, 0)
    start(1, 1)
    if not has_start:
        canvas[COL_PAD : COL_PAD + QUARTER_COLS, row_pad : row_pad + rows, :] = jnp.zeros(
            (QUARTER_COLS, rows, LANES), jnp.float32
        )
    for load in loads:
        load.wait()

    def place(i):
        k = chosen[i]
        stripe_at, rho, col = corner(k)
        col_tile = col >> 7
        shift = col & (LANES - 1)
        parted = ((stripe_at + core) & 1) == 0
        slot_row = stripe * ((stripe_at + 1 - core) >> 1)
        first = jnp.where(parted, 2 * stripe - rho, stripe - rho)
        first_at = pl.multiple_of((first >> 4) << 4, PAD)
        delta = first - first_at
        return k, rho, col_tile, shift, parted, slot_row, first_at, delta

    def down_pass(info, slot, half):
        k, first_at = info[0], info[6]
        kernel = index_ref[k]
        scales = [table_ref[b, kernel] * weight_ref[k] for b in range(BASES)]
        for g in range(groups):
            for part in range(parts):
                at = pl.multiple_of(g * group_rows + first_at + part * height, PAD)
                result = jnp.dot(
                    down_ref[...],
                    tile_buf[slot, pl.ds(at, height + 2 * PAD), :],
                    preferred_element_type=jnp.float32,
                )
                for b in range(BASES):
                    spread[
                        half * groups + g,
                        part * height : (part + 1) * height,
                        b * BLOCK : (b + 1) * BLOCK,
                    ] = (result[b * height : (b + 1) * height] * scales[b]).astype(jnp.bfloat16)

    def across_pass(info, half):
        k, rho, col_tile, shift, parted, slot_row, first_at, delta = info
        lane = lax.broadcasted_iota(jnp.int32, (window, LANES), 1)
        local = lax.broadcasted_iota(jnp.int32, (window, LANES), 0) - delta
        split_at = jnp.where(parted, rho, stripe)
        last = jnp.where(parted, stripe + gap, stripe)
        valid = (local >= 0) & (
            (local < split_at) | ((local >= rho + gap) & (local < last))
        )
        for g in range(groups):
            wide = []
            for side in range(3):
                acc = None
                for b in range(BASES):
                    lo = LANES * side
                    term = jnp.dot(
                        spread[half * groups + g, :, b * BLOCK + lo : b * BLOCK + lo + 256],
                        band_ref[b * BLOCK + lo : b * BLOCK + lo + 256, 256 * side : 256 * side + 256],
                        preferred_element_type=jnp.float32,
                    )
                    acc = term if acc is None else acc + term
                wide.append(acc)
            merged = jnp.concatenate(
                [
                    wide[0][:, :LANES],
                    wide[0][:, LANES:] + wide[1][:, :LANES],
                    wide[1][:, LANES:] + wide[2][:, :LANES],
                    wide[2][:, LANES:],
                ],
                axis=1,
            )
            turned = [
                pltpu.roll(merged[:, j * LANES : (j + 1) * LANES], shift, 1)
                for j in range(COL_PAD)
            ]
            base = row_pad + slot_row + g * stripe - delta
            upper_at = jnp.where(parted, base + stripe, base)
            lower_at = jnp.where(parted, base - gap, base)
            pieces = []
            for j in range(COL_PAD + 1):
                left = turned[j - 1] if j > 0 else 0.0
                right = turned[j] if j < COL_PAD else 0.0
                pieces.append(jnp.where(valid, jnp.where(lane < shift, left, right), 0.0))
            for top in range(0, window, 8 * BATCH):
                spots, sums = [], []
                for row in range(top, min(top + 8 * BATCH, window), 8):
                    at = row + jnp.where(row < split_at + delta, upper_at, lower_at)
                    for j in range(COL_PAD + 1):
                        spot = (col_tile + j, pl.ds(at, 8), slice(None))
                        spots.append(spot)
                        sums.append(canvas[spot] + pieces[j][row : row + 8])
                for spot, value in zip(spots, sums):
                    canvas[spot] = value

    def pair(n, carry):
        slot = 2 * (n & 1)
        start(2 * n + 2, 2 - slot)
        start(2 * n + 3, 3 - slot)
        infos = [place(2 * n), place(2 * n + 1)]
        for half in range(2):
            fetch(2 * n + half, slot + half, lambda copy: copy.wait())
        for half in range(2):
            down_pass(infos[half], slot + half, half)
        for half in range(2):
            across_pass(infos[half], half)
        return carry

    lax.fori_loop(0, count >> 1, pair, 0)

    @pl.when((count & 1) == 1)
    def _():
        last = count - 1
        slot = last & 3
        info = place(last)
        fetch(last, slot, lambda copy: copy.wait())
        down_pass(info, slot, 0)
        across_pass(info, 0)

    if not split:
        stores = canvas_copies(outs[0], True)
        for store in stores:
            store.start()
        for store in stores:
            store.wait()
        return

    mixed = slots == 2
    stores = []
    for kind, out in enumerate(outs):
        for i in range(slots):
            slot = row_at ^ (slots - 1 - i)
            side = col_at if kind == 1 else 1 - col_at
            if mixed:
                odd = core == 1
                slot = jnp.where(odd, row_at ^ (1 - kind), slot)
                side = jnp.where(odd, col_at ^ (1 - i), side)
            at = pl.multiple_of(row_pad + slot * stripe, PAD)
            for j in range(TILE_COLS):
                piece = canvas[COL_PAD + side * TILE_COLS + j, pl.ds(at, stripe), :]
                stages[kind][i, :, j * LANES : (j + 1) * LANES] = piece.astype(out.dtype)
            place_out = out.at[pl.ds(i * stripe, stripe)]
            store = pltpu.make_async_copy(
                stages[kind].at[i], place_out, side_sems.at[kind * slots + i]
            )
            store.start()
            stores.append(store)
    for store in stores:
        store.wait()


def make_quarter(geom, step, table, images, lists, bands, start=None, split=True, after=(), fields=None):
    stripe, slots = geom
    groups, gap, window, parts, group_rows, row_pad = geometry(stripe)
    rows = slots * stripe
    smem = pl.BlockSpec(memory_space=pltpu.SMEM)
    hbm = pl.BlockSpec(memory_space=pl.ANY)
    sources = len(images)
    has_start = start is not None
    extra = 0 if fields is None else FIELD_ROWS
    if split:
        out_shape = [
            jax.ShapeDtypeStruct((rows + extra, SIDE), jnp.bfloat16),
            jax.ShapeDtypeStruct((rows, SIDE), jnp.float32),
        ]
    else:
        out_shape = [jax.ShapeDtypeStruct((QUARTER_COLS, rows, LANES), jnp.float32)]
    stages = [pltpu.VMEM((slots, stripe, SIDE), item.dtype) for item in out_shape] if split else []
    token = jax.ShapeDtypeStruct((1, 1), jnp.float32)
    return pl.pallas_call(
        functools.partial(quarter_kernel, geom, step, sources, has_start, split, len(after), fields is not None),
        out_shape=out_shape + [token],
        in_specs=[smem] * 5
        + [hbm] * sources
        + [hbm, hbm]
        + ([hbm] if has_start else [])
        + [hbm] * (len(after) + (fields is not None)),
        out_specs=[hbm] * len(out_shape) + [smem],
        scratch_shapes=[
            pltpu.VMEM((COL_TILES, 2 * row_pad + rows, LANES), jnp.float32),
            pltpu.VMEM((4, groups * group_rows, BLOCK), jnp.bfloat16),
            pltpu.VMEM((2 * groups, window, BASES * BLOCK), jnp.bfloat16),
            pltpu.VMEM(bands[0].shape, jnp.bfloat16),
            pltpu.VMEM(bands[1].shape, jnp.bfloat16),
            pltpu.SMEM((sources * images[0].shape[0] + 1,), jnp.int32),
            pltpu.SemaphoreType.DMA((4, 2 * groups)),
            pltpu.SemaphoreType.DMA((max(7, 2 * slots),)),
        ]
        + stages,
        compiler_params=pltpu.CompilerParams(vmem_limit_bytes=60 * 1024 * 1024),
        cost_estimate=pl.CostEstimate(flops=1 << 20, bytes_accessed=1 << 20, transcendentals=0),
    )(table, *lists, *images, *bands, *([start] if has_start else []), *after, *([] if fields is None else [fields]))


def on_device(
    expo_count, patch_count, images, block_weight, block_patch, block_offset, kernel_index, coef_table
):
    stripe = SIDE // expo_count
    slots = expo_count // 2
    depth = patch_count // 2
    mixed = slots == 2
    expo, patch = lax.axis_index("expo"), lax.axis_index("patch")
    everyone = [(e, p) for e in range(expo_count) for p in range(patch_count)]

    def swap(value, partner):
        route = []
        for e, p in everyone:
            to_e, to_p = partner(e, p)
            route.append((e * patch_count + p, to_e * patch_count + to_p))
        return lax.ppermute(value, ("expo", "patch"), route)

    def twin(e, p):
        return e ^ 1, p

    def first_partner(e, p):
        if mixed and e % 2 == 1:
            return e ^ 2, p
        return e, p ^ 1

    twin_images = swap(images, twin)
    weights = block_weight.astype(jnp.float32)
    own = (block_patch.T, block_offset.T, kernel_index, weights)
    lists = jnp.stack(
        [block_patch[:, 0], block_offset[:, 0], block_offset[:, 1], kernel_index]
    ).astype(jnp.float32)
    lists = jnp.concatenate([lists, weights[None]], axis=0)
    twin_lists = swap(lists, twin)
    lists = jnp.concatenate([lists, twin_lists], axis=1)

    def unpack(known):
        ids = known[:4].astype(jnp.int32)
        return ids[:1], ids[1:3], ids[3], known[4]

    other, both = unpack(twin_lists), unpack(lists)

    ids = lists[:3].astype(jnp.int32)
    top = (ids[0] // PGX) * SIDE + ids[1]
    left = (ids[0] % PGX) * SIDE + ids[2]
    digits = jnp.stack([top // LANES, top % LANES, left // LANES, left % LANES])
    fields = jnp.concatenate([digits.astype(jnp.bfloat16), lists[4:].astype(jnp.bfloat16)], axis=0)

    def full(known):
        return jnp.pad(known, ((0, FIELD_ROWS - known.shape[0]), (0, SIDE - known.shape[1])))

    def below(value, known):
        return value if known is None else jnp.concatenate([value, full(known)], axis=0)

    def known_in(value, count):
        return value[-FIELD_ROWS:][: fields.shape[0], :count]

    table = coef_table.T
    bands = make_bands(stripe)

    def quarter(step, *args, **kwargs):
        return make_quarter((stripe, slots), step, table, *args, **kwargs)

    def second_hops(stay, got, token, known):
        def add(n):
            rows = slice(n * stripe, (n + 1) * stripe)
            return stay[rows] + got[rows].astype(jnp.float32)

        total = add(slots - 1)
        parts = [
            below((add(slots - 1 - hop) + token).astype(jnp.bfloat16), known)
            for hop in range(1, slots)
        ]
        return total, parts

    def second_swap(parts):
        received = []
        for hop, part in enumerate(parts, 1):

            def partner(e, p, hop=hop):
                if mixed and e % 2 == 1:
                    return e, p ^ 1
                return e ^ (2 * hop), p

            received.append(swap(part, partner))
        return received

    steps = list(range(depth))[::-1]
    early = quarter(
        steps[0], [images], own, bands, split=False
    )[0]
    leave, stay, _ = quarter(
        steps[0], [twin_images], other, bands, start=early, fields=full(fields)
    )

    def finish(entry, token=0.0):
        _, total, received = entry
        for value in received:
            total = total + value[:stripe].astype(jnp.float32)
        return total + token

    def advance(entry, token, known=None):
        number, kept, arrival = entry
        total, parts = second_hops(kept, arrival, token, known)
        return (number, total, second_swap(parts)), parts

    carried, neighbour = {}, []

    def forward(number, total, known=None):
        for value in carried.pop(number, []):
            total = total + value[:stripe].astype(jnp.float32)
        if number == 0:
            return total
        low = number & -number
        sent = below(total.astype(jnp.bfloat16), known)
        moved = swap(sent, lambda e, p: (e, p ^ (2 * low)))
        carried.setdefault(number ^ low, []).append(moved)
        if known is not None:
            neighbour.append(known_in(moved, known.shape[1]))
        return sent

    firsts, seconds, result, known = [], [], None, fields
    for step in steps:
        firsts.append((step, stay, swap(leave, first_partner)))
        if step == 0:
            break
        after = [leave]
        if len(firsts) > 1:
            if seconds:
                entry = seconds.pop(0)
                lists_now = None
                if entry[0] == depth - 1:
                    more = [known_in(value, known.shape[1]) for value in entry[2]]
                    known = lists_now = jnp.concatenate([known] + more, axis=1)
                after.append(forward(entry[0], finish(entry, token), lists_now))
            lists_now = None
            if firsts[0][0] == depth - 1:
                more = known_in(firsts[0][2], known.shape[1])
                known = lists_now = jnp.concatenate([known, more], axis=1)
            entry, parts = advance(firsts.pop(0), token, lists_now)
            seconds.append(entry)
            after += parts
        leave, stay, token = quarter(step - 1, [images, twin_images], both, bands, after=after)
        token = token[0, 0]
    known = jnp.concatenate([known] + neighbour, axis=1)
    while firsts or seconds:
        entry = seconds.pop(0)
        result = forward(entry[0], finish(entry, token))
        if firsts:
            seconds.append(advance(firsts.pop(0), token)[0])
    reach = 4
    while reach < patch_count:
        known = jnp.concatenate([known, swap(known, lambda e, p, r=reach: (e, p ^ r))], axis=1)
        reach *= 2

    places = known[:4].astype(jnp.int32)
    top = places[0] * LANES + places[1] - MARGIN
    left = places[2] * LANES + places[3] - MARGIN
    my_row = (patch // PGX) * SIDE + expo * stripe + jnp.arange(stripe)
    my_col = (patch % PGX) * SIDE + jnp.arange(SIDE)
    row_gap = my_row[:, None] - top[None, :]
    col_gap = my_col[None, :] - left[:, None]
    row_in = jnp.where((row_gap >= 0) & (row_gap < BLOCK), known[4][None, :], 0.0)
    col_in = (col_gap >= 0) & (col_gap < BLOCK)
    weight_map = jnp.dot(
        row_in.astype(jnp.bfloat16),
        col_in.astype(jnp.bfloat16),
        preferred_element_type=jnp.float32,
    )

    coadd_map = result / jnp.maximum(weight_map, weight_floor)
    return (coadd_map[None], weight_map[None])


def solution(mesh):
    return jax.shard_map(
        functools.partial(on_device, mesh.shape["expo"], mesh.shape["patch"]),
        mesh=mesh,
        in_specs=(
            P(("expo", "patch"), None, None),
            P(("expo", "patch")),
            P(("expo", "patch"), None),
            P(("expo", "patch"), None),
            P(("expo", "patch")),
            P(),
        ),
        out_specs=(P("patch", "expo", None), P("patch", "expo", None)),
        check_vma=False,
    )
```

```python
import functools

import jax
import jax.numpy as jnp
import ml_dtypes
import numpy as np
from jax import lax
from jax.experimental import pallas as pl
from jax.experimental.pallas import tpu as pltpu
from jax.sharding import PartitionSpec as P

BLOCK = 512
KHALF = 10
BASES = 3
SIDE = 1024
MARGIN = 128
PGX = 4
PGX_BITS = 2
SIGMAS = (0.8, 1.6, 3.2)
weight_floor = 0.5

LANES = 128
HALF = BLOCK // 2
PAD = 16
BATCH = 4
STREAMS = 2
NEW_META = True
FIELD_ROWS = 16
COL_PAD = BLOCK // LANES
TILE_COLS = SIDE // LANES
QUARTER_COLS = 2 * TILE_COLS
COL_TILES = QUARTER_COLS + 2 * COL_PAD


def taps_at(basis, distance):
    offsets = np.arange(-KHALF, KHALF + 1).astype(np.float32)
    taps = []
    for sigma in SIGMAS:
        profile = np.exp(-offsets * offsets / np.float32(2.0 * sigma * sigma))
        taps.append(profile / np.sum(profile, dtype=np.float32))
    taps = np.stack(taps).astype(ml_dtypes.bfloat16)
    inside = np.abs(distance) <= KHALF
    found = taps[basis, np.where(inside, distance + KHALF, 0)]
    return np.where(inside, found, np.zeros((), ml_dtypes.bfloat16))


def geometry(stripe):
    groups = HALF // stripe
    gap = PAD if groups == 1 else 2 * PAD
    window = stripe + PAD + gap
    parts = 2 if groups == 1 else 1
    group_rows = PAD + 2 * stripe + gap + stripe + 2 * PAD
    row_pad = HALF + PAD + gap
    return groups, gap, window, parts, group_rows, row_pad


def make_bands(stripe):
    _, _, window, parts, _, _ = geometry(stripe)
    height = window // parts
    row, col = np.indices((BASES * height, height + 2 * PAD))
    down = taps_at(row // height, col - row % height - PAD)
    row, col = np.indices((2 * LANES, 2 * LANES))
    across = []
    for side, (low, high) in enumerate(((0, 192), (192, 320), (320, BLOCK))):
        mine = (col + side * LANES >= low) & (col + side * LANES < high)
        for b in range(BASES):
            across.append(np.where(mine, taps_at(np.full_like(row, b), col - row), 0))
    across = np.concatenate(across, axis=0)
    return jnp.asarray(down, jnp.bfloat16), jnp.asarray(across, jnp.bfloat16)


def quarter_kernel(geom, step, sources, has_start, split, waits, has_fields, *refs):
    stripe, slots = geom
    groups, gap, window, parts, group_rows, row_pad = geometry(stripe)
    height = window // parts
    refs = list(refs)
    table_ref = refs.pop(0)
    lists = [(refs.pop(0), refs.pop(0)) for _ in range(sources)]
    images = [refs.pop(0) for _ in range(sources)]
    band_hbm = [refs.pop(0), refs.pop(0)]
    start_ref = refs.pop(0) if has_start else None
    refs = refs[waits:]
    fields_ref = refs.pop(0) if has_fields else None
    outs = [refs.pop(0) for _ in range(2 if split else 1)]
    token_ref = refs.pop(0)
    canvas, tile_buf, spread, down_ref, band_ref, chosen, sems, side_sems = refs[:8]
    stages = refs[8:10]
    early_ref = refs[10] if has_start else None
    expo, place_at = lax.axis_index("expo"), lax.axis_index("patch")
    core, row_at, col_at, quarter = expo & 1, expo >> 1, place_at & 1, (place_at >> 1) ^ step
    rows = slots * stripe
    per_source = images[0].shape[0]

    def canvas_copies(other, out):
        copies = []
        for n in range(4):
            cols = pl.ds(n * (QUARTER_COLS // 4), QUARTER_COLS // 4)
            far = other.at[cols]
            if out:
                mine = canvas.at[pl.ds(COL_PAD + cols.start, cols.size), pl.ds(row_pad, rows), :]
                copies.append(pltpu.make_async_copy(mine, far, side_sems.at[2 + n]))
            else:
                copies.append(pltpu.make_async_copy(far, early_ref.at[cols], side_sems.at[2 + n]))
        return copies

    late = []
    third = band_ref.shape[0] // 3
    loads = [pltpu.make_async_copy(band_hbm[0], down_ref, side_sems.at[0])]
    for n in range(3):
        part = pl.ds(n * third, third)
        loads.append(
            pltpu.make_async_copy(band_hbm[1].at[part], band_ref.at[part], side_sems.at[7 + n])
        )
    if has_start:
        late = canvas_copies(start_ref, False)
    if has_fields:
        loads.append(
            pltpu.make_async_copy(
                fields_ref, outs[0].at[pl.ds(rows, FIELD_ROWS)], side_sems.at[6]
            )
        )
    token_ref[0, 0] = 0.0
    for load in loads + late:
        load.start()

    stripe_bits = stripe.bit_length() - 1
    row_shift = BLOCK - MARGIN - (quarter >> 1) * SIDE
    col_shift = BLOCK - MARGIN - (quarter & 1) * (2 * SIDE)

    def located(top, left):
        row, col = top + row_shift, left + col_shift
        return (row >> stripe_bits) - BLOCK // stripe, row & (stripe - 1), col

    def look_up(k, pick):
        value = pick(lists[0], jnp.minimum(k, per_source - 1))
        for n in range(1, sources):
            other = pick(lists[n], jnp.maximum(k - n * per_source, 0))
            value = jnp.where(k < n * per_source, value, other)
        return value

    def entry(k, field):
        return look_up(k, lambda item, i: item[0][field, i])

    count = jnp.int32(0)
    for n, (place_ref, _) in enumerate(lists):

        def scan(i, count, n=n, place_ref=place_ref):
            stripe_at, rho, col = located(place_ref[0, i], place_ref[1, i])
            lowest = jnp.maximum(stripe_at, 0)
            lowest = lowest + ((lowest + core) & 1)
            highest = stripe_at + BLOCK // stripe - (rho == 0).astype(jnp.int32)
            hit = (lowest <= jnp.minimum(highest, 2 * slots - 1)) & (col > 0)
            hit = hit & (col < BLOCK + 2 * SIDE)
            chosen[count] = i + n * per_source
            return count + hit.astype(jnp.int32)

        count = lax.fori_loop(0, per_source, scan, count)

    def pieces_of(g):
        top, base = 2 * stripe * g, group_rows * g
        early = PAD if g > 0 else 0
        late = PAD if g < groups - 1 else 0
        again = base + PAD + 2 * stripe + gap
        return [
            (top - early, early + 2 * stripe + late, base + PAD - early),
            (top - early, early + stripe + PAD, again - early),
        ]

    def fetch(i, slot, act):
        k = chosen[i]
        for n, image_ref in enumerate(images):

            @pl.when((k >= n * per_source) & (k < (n + 1) * per_source))
            def _():
                for g in range(groups):
                    for c, (top, size, to) in enumerate(pieces_of(g)):
                        act(
                            pltpu.make_async_copy(
                                image_ref.at[k - n * per_source, pl.ds(top, size), :],
                                tile_buf.at[slot, pl.ds(to, size), :],
                                sems.at[slot, 2 * g + c],
                            )
                        )

    def start(i, slot):
        @pl.when(i < count)
        def _():
            fetch(i, slot, lambda copy: copy.start())

    for slot in range(4):
        for g in range(groups):
            base = group_rows * g
            again = base + PAD + 2 * stripe + gap
            for top, bottom in (
                (base, base + PAD),
                (base + PAD + 2 * stripe, again),
                (again + stripe + PAD, base + group_rows),
            ):
                tile_buf[slot, top:bottom, :] = jnp.zeros((bottom - top, BLOCK), tile_buf.dtype)
    start(0, 0)
    start(1, 1)
    canvas[COL_PAD : COL_PAD + QUARTER_COLS, row_pad : row_pad + rows, :] = jnp.zeros(
        (QUARTER_COLS, rows, LANES), jnp.float32
    )
    for load in loads:
        load.wait()

    def place(i):
        k = chosen[i]
        stripe_at, rho, col = located(entry(k, 0), entry(k, 1))
        col_tile = col >> 7
        shift = col & (LANES - 1)
        parted = ((stripe_at + core) & 1) == 0
        slot_row = stripe * ((stripe_at + 1 - core) >> 1)
        first = jnp.where(parted, 2 * stripe - rho, stripe - rho)
        first_at = pl.multiple_of((first >> 4) << 4, PAD)
        delta = first - first_at
        return k, rho, col_tile, shift, parted, slot_row, first_at, delta

    def down_pass(info, slot, half):
        k, first_at = info[0], info[6]
        kernel = entry(k, 2)
        weight = look_up(k, lambda item, i: item[1][i])
        scales = [table_ref[b, kernel] * weight for b in range(BASES)]
        for g in range(groups):
            for part in range(parts):
                at = pl.multiple_of(g * group_rows + first_at + part * height, PAD)
                result = jnp.dot(
                    down_ref[...],
                    tile_buf[slot, pl.ds(at, height + 2 * PAD), :],
                    preferred_element_type=jnp.float32,
                )
                for b in range(BASES):
                    spread[
                        half * groups + g,
                        part * height : (part + 1) * height,
                        b * BLOCK : (b + 1) * BLOCK,
                    ] = (result[b * height : (b + 1) * height] * scales[b]).astype(jnp.bfloat16)

    def across_pass(info, half):
        k, rho, col_tile, shift, parted, slot_row, first_at, delta = info
        lane = lax.broadcasted_iota(jnp.int32, (window, LANES), 1)
        local = lax.broadcasted_iota(jnp.int32, (window, LANES), 0) - delta
        split_at = jnp.where(parted, rho, stripe)
        last = jnp.where(parted, stripe + gap, stripe)
        valid = (local >= 0) & (
            (local < split_at) | ((local >= rho + gap) & (local < last))
        )
        for g in range(groups):
            wide = []
            for side in range(3):
                acc = None
                for b in range(BASES):
                    lo = b * BLOCK + LANES * side
                    at = (side * BASES + b) * 2 * LANES
                    term = jnp.dot(
                        spread[half * groups + g, :, lo : lo + 2 * LANES],
                        band_ref[at : at + 2 * LANES],
                        preferred_element_type=jnp.float32,
                    )
                    acc = term if acc is None else acc + term
                wide.append(acc)
            merged = jnp.concatenate(
                [
                    wide[0][:, :LANES],
                    wide[0][:, LANES:] + wide[1][:, :LANES],
                    wide[1][:, LANES:] + wide[2][:, :LANES],
                    wide[2][:, LANES:],
                ],
                axis=1,
            )
            turned = [
                pltpu.roll(merged[:, j * LANES : (j + 1) * LANES], shift, 1)
                for j in range(COL_PAD)
            ]
            base = row_pad + slot_row + g * stripe - delta
            upper_at = jnp.where(parted, base + stripe, base)
            lower_at = jnp.where(parted, base - gap, base)
            pieces = []
            for j in range(COL_PAD + 1):
                left = turned[j - 1] if j > 0 else 0.0
                right = turned[j] if j < COL_PAD else 0.0
                pieces.append(jnp.where(valid, jnp.where(lane < shift, left, right), 0.0))
            for top in range(0, window, 8 * BATCH):
                spots, sums = [], []
                for row in range(top, min(top + 8 * BATCH, window), 8):
                    at = row + jnp.where(row < split_at + delta, upper_at, lower_at)
                    for j in range(COL_PAD + 1):
                        spot = (col_tile + j, pl.ds(at, 8), slice(None))
                        spots.append(spot)
                        sums.append(canvas[spot] + pieces[j][row : row + 8])
                for spot, value in zip(spots, sums):
                    canvas[spot] = value

    def pair(n, carry):
        slot = 2 * (n & 1)
        start(2 * n + 2, 2 - slot)
        start(2 * n + 3, 3 - slot)
        infos = [place(2 * n), place(2 * n + 1)]
        for half in range(2):
            fetch(2 * n + half, slot + half, lambda copy: copy.wait())
        for half in range(2):
            down_pass(infos[half], slot + half, half)
        for half in range(2):
            across_pass(infos[half], half)
        return carry

    lax.fori_loop(0, count >> 1, pair, 0)

    @pl.when((count & 1) == 1)
    def _():
        last = count - 1
        slot = last & 3
        info = place(last)
        fetch(last, slot, lambda copy: copy.wait())
        down_pass(info, slot, 0)
        across_pass(info, 0)

    if not split:
        stores = canvas_copies(outs[0], True)
        for store in stores:
            store.start()
        for store in stores:
            store.wait()
        return

    for load in late:
        load.wait()
    mixed = slots == 2
    stores = []
    for kind, out in enumerate(outs):
        for i in range(slots):
            slot = row_at ^ (slots - 1 - i)
            side = col_at if kind == 1 else 1 - col_at
            if mixed:
                odd = core == 1
                slot = jnp.where(odd, row_at ^ (1 - kind), slot)
                side = jnp.where(odd, col_at ^ (1 - i), side)
            at = pl.multiple_of(row_pad + slot * stripe, PAD)
            for j in range(TILE_COLS):
                piece = canvas[COL_PAD + side * TILE_COLS + j, pl.ds(at, stripe), :]
                if has_start:
                    from_row = pl.multiple_of(slot * stripe, stripe)
                    piece = piece + early_ref[side * TILE_COLS + j, pl.ds(from_row, stripe), :]
                stages[kind][i, :, j * LANES : (j + 1) * LANES] = piece.astype(out.dtype)
            for n in range(STREAMS):
                size = stripe // STREAMS
                store = pltpu.make_async_copy(
                    stages[kind].at[i, pl.ds(n * size, size)],
                    out.at[pl.ds(i * stripe + n * size, size)],
                    side_sems.at[10 + (kind * slots + i) * STREAMS + n],
                )
                store.start()
                stores.append(store)
    for store in stores:
        store.wait()


def make_quarter(geom, step, table, images, lists, bands, start=None, split=True, after=(), fields=None):
    stripe, slots = geom
    groups, gap, window, parts, group_rows, row_pad = geometry(stripe)
    rows = slots * stripe
    smem = pl.BlockSpec(memory_space=pltpu.SMEM)
    hbm = pl.BlockSpec(memory_space=pl.ANY)
    sources = len(images)
    has_start = start is not None
    extra = 0 if fields is None else FIELD_ROWS
    if split:
        out_shape = [
            jax.ShapeDtypeStruct((rows + extra, SIDE), jnp.bfloat16),
            jax.ShapeDtypeStruct((rows, SIDE), jnp.float32),
        ]
    else:
        out_shape = [jax.ShapeDtypeStruct((QUARTER_COLS, rows, LANES), jnp.float32)]
    stages = [pltpu.VMEM((slots, stripe, SIDE), item.dtype) for item in out_shape] if split else []
    token = jax.ShapeDtypeStruct((1, 1), jnp.float32)
    return pl.pallas_call(
        functools.partial(quarter_kernel, geom, step, sources, has_start, split, len(after), fields is not None),
        out_shape=out_shape + [token],
        in_specs=[smem] * (1 + 2 * sources)
        + [hbm] * sources
        + [hbm, hbm]
        + ([hbm] if has_start else [])
        + [hbm] * (len(after) + (fields is not None)),
        out_specs=[hbm] * len(out_shape) + [smem],
        scratch_shapes=[
            pltpu.VMEM((COL_TILES, 2 * row_pad + rows, LANES), jnp.float32),
            pltpu.VMEM((4, groups * group_rows, BLOCK), jnp.bfloat16),
            pltpu.VMEM((2 * groups, window, BASES * BLOCK), jnp.bfloat16),
            pltpu.VMEM(bands[0].shape, jnp.bfloat16),
            pltpu.VMEM(bands[1].shape, jnp.bfloat16),
            pltpu.SMEM((sources * images[0].shape[0] + 1,), jnp.int32),
            pltpu.SemaphoreType.DMA((4, 2 * groups)),
            pltpu.SemaphoreType.DMA((10 + STREAMS * 2 * slots,)),
        ]
        + stages
        + ([pltpu.VMEM((QUARTER_COLS, rows, LANES), jnp.float32)] if has_start else []),
        compiler_params=pltpu.CompilerParams(vmem_limit_bytes=63 * 1024 * 1024),
        cost_estimate=pl.CostEstimate(flops=1 << 20, bytes_accessed=1 << 20, transcendentals=0),
    )(table, *lists, *images, *bands, *([start] if has_start else []), *after, *([] if fields is None else [fields]))


def merge(stripe, jobs, after=()):
    halves = 2
    size = stripe // halves
    operands, plan = [], []
    for base, row, addends, known in jobs:
        plan.append((len(operands), row, [start for _, start in addends], known is not None))
        operands += [base] + [value for value, _ in addends] + ([] if known is None else [known])
    count = sum(1 + len(starts) for _, _, starts, _ in plan)

    def kernel(*refs):
        inputs = refs[: len(operands)]
        outs = refs[len(operands) + len(after) :][: len(jobs)]
        token_ref = refs[len(operands) + len(after) + len(jobs)]
        scratch = refs[len(operands) + len(after) + len(jobs) + 1 :]
        wide, narrow, staged, sems, out_sems = scratch
        token_ref[0, 0] = 0.0
        copies, lists, which, where = [], [], 0, 0
        for n, (at, row, starts, has_known) in enumerate(plan):
            sources = [(inputs[at], row, wide.at[n])]
            for m, start in enumerate(starts):
                sources.append((inputs[at + 1 + m], start, narrow.at[where + m]))
            where += len(starts)
            per_half = []
            for h in range(halves):
                group = []
                for m, (ref, start, to) in enumerate(sources):
                    copy = pltpu.make_async_copy(
                        ref.at[pl.ds(start + h * size, size)],
                        to.at[pl.ds(h * size, size)],
                        sems.at[which + m, h],
                    )
                    copy.start()
                    group.append(copy)
                per_half.append(group)
            which += len(sources)
            copies.append(per_half)
            if has_known:
                lists.append(
                    pltpu.make_async_copy(
                        inputs[at + 1 + len(starts)],
                        outs[n].at[pl.ds(stripe, FIELD_ROWS)],
                        out_sems.at[n, halves],
                    )
                )
                lists[-1].start()
        where = 0
        for n, (at, row, starts, has_known) in enumerate(plan):
            for h in range(halves):
                for copy in copies[n][h]:
                    copy.wait()
                rows = pl.ds(h * size, size)
                total = wide[n, rows, :]
                for m in range(len(starts)):
                    total = total + narrow[where + m, rows, :].astype(jnp.float32)
                staged[n, rows, :] = total.astype(jnp.bfloat16)
                store = pltpu.make_async_copy(
                    staged.at[n, rows], outs[n].at[rows], out_sems.at[n, h]
                )
                store.start()
                lists.append(store)
            where += len(starts)
        for copy in lists:
            copy.wait()

    hbm = pl.BlockSpec(memory_space=pl.ANY)
    shapes = [
        jax.ShapeDtypeStruct((stripe + (FIELD_ROWS if has_known else 0), SIDE), jnp.bfloat16)
        for _, _, _, has_known in plan
    ]
    out = pl.pallas_call(
        kernel,
        out_shape=shapes + [jax.ShapeDtypeStruct((1, 1), jnp.float32)],
        in_specs=[hbm] * (len(operands) + len(after)),
        out_specs=[hbm] * len(shapes) + [pl.BlockSpec(memory_space=pltpu.SMEM)],
        scratch_shapes=[
            pltpu.VMEM((len(jobs), stripe, SIDE), jnp.float32),
            pltpu.VMEM((count - len(jobs), stripe, SIDE), jnp.bfloat16),
            pltpu.VMEM((len(jobs), stripe, SIDE), jnp.bfloat16),
            pltpu.SemaphoreType.DMA((count, halves)),
            pltpu.SemaphoreType.DMA((len(jobs), halves + 1)),
        ],
        compiler_params=pltpu.CompilerParams(vmem_limit_bytes=63 * 1024 * 1024),
        cost_estimate=pl.CostEstimate(flops=0, bytes_accessed=0, transcendentals=0),
    )(*operands, *after)
    return out[: len(jobs)], out[-1][0, 0]


def on_device(
    expo_count, patch_count, images, block_weight, block_patch, block_offset, kernel_index, coef_table
):
    stripe = SIDE // expo_count
    slots = expo_count // 2
    depth = patch_count // 2
    mixed = slots == 2
    expo, patch = lax.axis_index("expo"), lax.axis_index("patch")
    everyone = [(e, p) for e in range(expo_count) for p in range(patch_count)]

    def swap(value, partner):
        route = []
        for e, p in everyone:
            to_e, to_p = partner(e, p)
            route.append((e * patch_count + p, to_e * patch_count + to_p))
        return lax.ppermute(value, ("expo", "patch"), route)

    def twin(e, p):
        return e ^ 1, p

    def first_partner(e, p):
        if mixed and e % 2 == 1:
            return e ^ 2, p
        return e, p ^ 1

    twin_images = swap(images, twin)
    weights = block_weight.astype(jnp.float32)
    places = jnp.stack(
        [
            (block_patch[:, 0] // PGX) * SIDE + block_offset[:, 0],
            (block_patch[:, 0] % PGX) * SIDE + block_offset[:, 1],
            kernel_index,
        ]
    )
    own = (places, weights)
    other = (swap(places, twin), swap(weights, twin))
    both = own + other
    table = coef_table.T
    bands = make_bands(stripe)

    def digits(places, weights):
        parts = [places[0] // LANES, places[0] % LANES, places[1] // LANES, places[1] % LANES]
        return jnp.stack([part.astype(jnp.bfloat16) for part in parts] + [weights.astype(jnp.bfloat16)])

    fields = jnp.concatenate([digits(*own), digits(*other)], axis=1)

    def full(known):
        return jnp.pad(known, ((0, FIELD_ROWS - known.shape[0]), (0, SIDE - known.shape[1])))

    def known_in(value, count):
        return value[-FIELD_ROWS:][: fields.shape[0], :count]

    table = coef_table.T
    bands = make_bands(stripe)

    def quarter(step, *args, **kwargs):
        return make_quarter((stripe, slots), step, table, *args, **kwargs)

    def own_job(entry, extra, known=None):
        _, stay, got, received = entry
        row = (slots - 1) * stripe
        addends = [(got, row)] + [(value, 0) for value in received + extra]
        return stay, row, addends, None if known is None else full(known)

    def part_jobs(entry, known=None):
        _, stay, got, _ = entry
        jobs = []
        for hop in range(1, slots):
            row = (slots - 1 - hop) * stripe
            jobs.append((stay, row, [(got, row)], None if known is None else full(known)))
        return jobs

    def second_swap(entry, parts):
        for hop, part in enumerate(parts, 1):

            def partner(e, p, hop=hop):
                if mixed and e % 2 == 1:
                    return e, p ^ 1
                return e ^ (2 * hop), p

            entry[3].append(swap(part, partner))

    carried = {}

    def forward(step, sent):
        low = step & -step
        moved = swap(sent, lambda e, p: (e, p ^ (2 * low)))
        carried.setdefault(step ^ low, []).append(moved)
        return moved

    steps = list(range(depth))[::-1]
    early = quarter(
        steps[0], [images], own, bands, split=False
    )[0]
    leave, stay, _ = quarter(
        steps[0], [twin_images], other, bands, start=early, fields=full(fields)
    )

    known, entries, moved = fields, [], {}

    def add_lists(values):
        return jnp.concatenate([known] + [known_in(v, known.shape[1]) for v in values], axis=1)

    def send_on(done, entry, after, lists_done=None, lists_entry=None):
        jobs = [] if done is None else [own_job(done, carried.get(done[0], []), lists_done)]
        sums, token = merge(stripe, jobs + part_jobs(entry, lists_entry), after)
        if done is not None:
            moved[done[0]] = forward(done[0], sums[0])
        second_swap(entry, sums[len(jobs) :])
        return sums, token

    for n, step in enumerate(steps):
        entries.append([step, stay, swap(leave, first_partner), []])
        after = [leave]
        if n == 1:
            known = add_lists([entries[0][2]])
            after += send_on(None, entries[0], after, None, known)[0]
        elif n > 1:
            done, lists_now = entries[n - 2], None
            if n < 4:
                known = lists_now = add_lists(done[3] if n == 2 else carried[done[0]][:1])
            after += send_on(done, entries[n - 1], after, lists_now)[0]
        if step:
            leave, stay, _ = quarter(step - 1, [images, twin_images], both, bands, after=after)
    done, entry = entries[-2:]
    sums, _ = merge(stripe, [own_job(done, carried.get(done[0], []))])
    moved[done[0]] = forward(done[0], sums[0])
    _, token = send_on(None, entry, sums)
    known = add_lists([moved[depth - 2]]) + token.astype(jnp.bfloat16)
    reach = 8
    while reach < patch_count:
        known = jnp.concatenate([known, swap(known, lambda e, p, r=reach: (e, p ^ r))], axis=1)
        reach *= 2

    base, row, addends, _ = own_job(entries[-1], carried[0])
    result = base[row : row + stripe]
    for value, start in addends:
        if value is addends[-1][0]:
            result = lax.optimization_barrier(result)
        result = result + value[start : start + stripe].astype(jnp.float32)

    places = known[:4].astype(jnp.int32)
    top = places[0] * LANES + places[1] - MARGIN
    left = places[2] * LANES + places[3] - MARGIN
    my_row = (patch // PGX) * SIDE + expo * stripe + jnp.arange(stripe)
    my_col = (patch % PGX) * SIDE + jnp.arange(SIDE)
    row_gap = my_row[:, None] - top[None, :]
    col_gap = my_col[None, :] - left[:, None]
    row_in = jnp.where((row_gap >= 0) & (row_gap < BLOCK), known[4][None, :], 0.0)
    col_in = (col_gap >= 0) & (col_gap < BLOCK)
    weight_map = jnp.dot(
        row_in.astype(jnp.bfloat16),
        col_in.astype(jnp.bfloat16),
        preferred_element_type=jnp.float32,
    )

    coadd_map = result / jnp.maximum(weight_map, weight_floor)
    return (coadd_map[None], weight_map[None])


def solution(mesh):
    return jax.shard_map(
        functools.partial(on_device, mesh.shape["expo"], mesh.shape["patch"]),
        mesh=mesh,
        in_specs=(
            P(("expo", "patch"), None, None),
            P(("expo", "patch")),
            P(("expo", "patch"), None),
            P(("expo", "patch"), None),
            P(("expo", "patch")),
            P(),
        ),
        out_specs=(P("patch", "expo", None), P("patch", "expo", None)),
        check_vma=False,
    )
```

```python
import functools

import jax
import jax.numpy as jnp
import ml_dtypes
import numpy as np
from jax import lax
from jax.experimental import pallas as pl
from jax.experimental.pallas import tpu as pltpu
from jax.sharding import PartitionSpec as P

BLOCK = 512
KHALF = 10
BASES = 3
SIDE = 1024
MARGIN = 128
PGX = 4
PGX_BITS = 2
SIGMAS = (0.8, 1.6, 3.2)
weight_floor = 0.5

LANES = 128
HALF = BLOCK // 2
PAD = 16
BATCH = 4
STREAMS = 2
NEW_META = True
FIELD_ROWS = 16
COL_PAD = BLOCK // LANES
TILE_COLS = SIDE // LANES
QUARTER_COLS = 2 * TILE_COLS
COL_TILES = QUARTER_COLS + 2 * COL_PAD


def taps_at(basis, distance):
    offsets = np.arange(-KHALF, KHALF + 1).astype(np.float32)
    taps = []
    for sigma in SIGMAS:
        profile = np.exp(-offsets * offsets / np.float32(2.0 * sigma * sigma))
        taps.append(profile / np.sum(profile, dtype=np.float32))
    taps = np.stack(taps).astype(ml_dtypes.bfloat16)
    inside = np.abs(distance) <= KHALF
    found = taps[basis, np.where(inside, distance + KHALF, 0)]
    return np.where(inside, found, np.zeros((), ml_dtypes.bfloat16))


def geometry(stripe):
    groups = HALF // stripe
    gap = PAD if groups == 1 else 2 * PAD
    window = stripe + PAD + gap
    parts = 2 if groups == 1 else 1
    group_rows = PAD + 2 * stripe + gap + stripe + 2 * PAD
    row_pad = HALF + PAD + gap
    return groups, gap, window, parts, group_rows, row_pad


def make_bands(stripe):
    _, _, window, parts, _, _ = geometry(stripe)
    height = window // parts
    row, col = np.indices((BASES * height, height + 2 * PAD))
    down = taps_at(row // height, col - row % height - PAD)
    row, col = np.indices((2 * LANES, 2 * LANES))
    across = []
    for side, (low, high) in enumerate(((0, 192), (192, 320), (320, BLOCK))):
        mine = (col + side * LANES >= low) & (col + side * LANES < high)
        for b in range(BASES):
            across.append(np.where(mine, taps_at(np.full_like(row, b), col - row), 0))
    across = np.concatenate(across, axis=0)
    return jnp.asarray(down, jnp.bfloat16), jnp.asarray(across, jnp.bfloat16)


def quarter_kernel(geom, step, sources, has_start, split, waits, has_fields, *refs):
    stripe, slots = geom
    groups, gap, window, parts, group_rows, row_pad = geometry(stripe)
    height = window // parts
    refs = list(refs)
    table_ref = refs.pop(0)
    lists = [(refs.pop(0), refs.pop(0)) for _ in range(sources)]
    images = [refs.pop(0) for _ in range(sources)]
    band_hbm = [refs.pop(0), refs.pop(0)]
    start_ref = refs.pop(0) if has_start else None
    refs = refs[waits:]
    fields_ref = refs.pop(0) if has_fields else None
    outs = [refs.pop(0) for _ in range(2 if split else 1)]
    token_ref = refs.pop(0)
    canvas, tile_buf, spread, down_ref, band_ref, chosen, sems, side_sems = refs[:8]
    stages = refs[8:10]
    early_ref = refs[10] if has_start else None
    expo, place_at = lax.axis_index("expo"), lax.axis_index("patch")
    core, row_at, col_at, quarter = expo & 1, expo >> 1, place_at & 1, (place_at >> 1) ^ step
    rows = slots * stripe
    per_source = images[0].shape[0]

    def canvas_copies(other, out):
        copies = []
        for n in range(4):
            cols = pl.ds(n * (QUARTER_COLS // 4), QUARTER_COLS // 4)
            far = other.at[cols]
            if out:
                mine = canvas.at[pl.ds(COL_PAD + cols.start, cols.size), pl.ds(row_pad, rows), :]
                copies.append(pltpu.make_async_copy(mine, far, side_sems.at[2 + n]))
            else:
                copies.append(pltpu.make_async_copy(far, early_ref.at[cols], side_sems.at[2 + n]))
        return copies

    late = []
    third = band_ref.shape[0] // 3
    loads = [pltpu.make_async_copy(band_hbm[0], down_ref, side_sems.at[0])]
    for n in range(3):
        part = pl.ds(n * third, third)
        loads.append(
            pltpu.make_async_copy(band_hbm[1].at[part], band_ref.at[part], side_sems.at[7 + n])
        )
    if has_start:
        late = canvas_copies(start_ref, False)
    if has_fields:
        loads.append(
            pltpu.make_async_copy(
                fields_ref, outs[0].at[pl.ds(rows, FIELD_ROWS)], side_sems.at[6]
            )
        )
    token_ref[0, 0] = 0.0
    for load in loads + late:
        load.start()

    stripe_bits = stripe.bit_length() - 1
    row_shift = BLOCK - MARGIN - (quarter >> 1) * SIDE
    col_shift = BLOCK - MARGIN - (quarter & 1) * (2 * SIDE)

    def located(top, left):
        row, col = top + row_shift, left + col_shift
        return (row >> stripe_bits) - BLOCK // stripe, row & (stripe - 1), col

    def look_up(k, pick):
        value = pick(lists[0], jnp.minimum(k, per_source - 1))
        for n in range(1, sources):
            other = pick(lists[n], jnp.maximum(k - n * per_source, 0))
            value = jnp.where(k < n * per_source, value, other)
        return value

    def entry(k, field):
        return look_up(k, lambda item, i: item[0][field, i])

    count = jnp.int32(0)
    for n, (place_ref, _) in enumerate(lists):

        def scan(i, count, n=n, place_ref=place_ref):
            stripe_at, rho, col = located(place_ref[0, i], place_ref[1, i])
            lowest = jnp.maximum(stripe_at, 0)
            lowest = lowest + ((lowest + core) & 1)
            highest = stripe_at + BLOCK // stripe - (rho == 0).astype(jnp.int32)
            hit = (lowest <= jnp.minimum(highest, 2 * slots - 1)) & (col > 0)
            hit = hit & (col < BLOCK + 2 * SIDE)
            chosen[count] = i + n * per_source
            return count + hit.astype(jnp.int32)

        count = lax.fori_loop(0, per_source, scan, count)

    def pieces_of(g):
        top, base = 2 * stripe * g, group_rows * g
        early = PAD if g > 0 else 0
        late = PAD if g < groups - 1 else 0
        again = base + PAD + 2 * stripe + gap
        return [
            (top - early, early + 2 * stripe + late, base + PAD - early),
            (top - early, early + stripe + PAD, again - early),
        ]

    def fetch(i, slot, act):
        k = chosen[i]
        for n, image_ref in enumerate(images):

            @pl.when((k >= n * per_source) & (k < (n + 1) * per_source))
            def _():
                for g in range(groups):
                    for c, (top, size, to) in enumerate(pieces_of(g)):
                        act(
                            pltpu.make_async_copy(
                                image_ref.at[k - n * per_source, pl.ds(top, size), :],
                                tile_buf.at[slot, pl.ds(to, size), :],
                                sems.at[slot, 2 * g + c],
                            )
                        )

    def start(i, slot):
        @pl.when(i < count)
        def _():
            fetch(i, slot, lambda copy: copy.start())

    for slot in range(4):
        for g in range(groups):
            base = group_rows * g
            again = base + PAD + 2 * stripe + gap
            for top, bottom in (
                (base, base + PAD),
                (base + PAD + 2 * stripe, again),
                (again + stripe + PAD, base + group_rows),
            ):
                tile_buf[slot, top:bottom, :] = jnp.zeros((bottom - top, BLOCK), tile_buf.dtype)
    start(0, 0)
    start(1, 1)
    canvas[COL_PAD : COL_PAD + QUARTER_COLS, row_pad : row_pad + rows, :] = jnp.zeros(
        (QUARTER_COLS, rows, LANES), jnp.float32
    )
    for load in loads:
        load.wait()

    def place(i):
        k = chosen[i]
        stripe_at, rho, col = located(entry(k, 0), entry(k, 1))
        col_tile = col >> 7
        shift = col & (LANES - 1)
        parted = ((stripe_at + core) & 1) == 0
        slot_row = stripe * ((stripe_at + 1 - core) >> 1)
        first = jnp.where(parted, 2 * stripe - rho, stripe - rho)
        first_at = pl.multiple_of((first >> 4) << 4, PAD)
        delta = first - first_at
        return k, rho, col_tile, shift, parted, slot_row, first_at, delta

    def down_pass(info, slot, half):
        k, first_at = info[0], info[6]
        kernel = entry(k, 2)
        weight = look_up(k, lambda item, i: item[1][i])
        scales = [table_ref[b, kernel] * weight for b in range(BASES)]
        for g in range(groups):
            for part in range(parts):
                at = pl.multiple_of(g * group_rows + first_at + part * height, PAD)
                result = jnp.dot(
                    down_ref[...],
                    tile_buf[slot, pl.ds(at, height + 2 * PAD), :],
                    preferred_element_type=jnp.float32,
                )
                for b in range(BASES):
                    spread[
                        half * groups + g,
                        part * height : (part + 1) * height,
                        b * BLOCK : (b + 1) * BLOCK,
                    ] = (result[b * height : (b + 1) * height] * scales[b]).astype(jnp.bfloat16)

    def across_pass(info, half):
        k, rho, col_tile, shift, parted, slot_row, first_at, delta = info
        lane = lax.broadcasted_iota(jnp.int32, (window, LANES), 1)
        local = lax.broadcasted_iota(jnp.int32, (window, LANES), 0) - delta
        split_at = jnp.where(parted, rho, stripe)
        last = jnp.where(parted, stripe + gap, stripe)
        valid = (local >= 0) & (
            (local < split_at) | ((local >= rho + gap) & (local < last))
        )
        for g in range(groups):
            wide = []
            for side in range(3):
                acc = None
                for b in range(BASES):
                    lo = b * BLOCK + LANES * side
                    at = (side * BASES + b) * 2 * LANES
                    term = jnp.dot(
                        spread[half * groups + g, :, lo : lo + 2 * LANES],
                        band_ref[at : at + 2 * LANES],
                        preferred_element_type=jnp.float32,
                    )
                    acc = term if acc is None else acc + term
                wide.append(acc)
            merged = jnp.concatenate(
                [
                    wide[0][:, :LANES],
                    wide[0][:, LANES:] + wide[1][:, :LANES],
                    wide[1][:, LANES:] + wide[2][:, :LANES],
                    wide[2][:, LANES:],
                ],
                axis=1,
            )
            turned = [
                pltpu.roll(merged[:, j * LANES : (j + 1) * LANES], shift, 1)
                for j in range(COL_PAD)
            ]
            base = row_pad + slot_row + g * stripe - delta
            upper_at = jnp.where(parted, base + stripe, base)
            lower_at = jnp.where(parted, base - gap, base)
            pieces = []
            for j in range(COL_PAD + 1):
                left = turned[j - 1] if j > 0 else 0.0
                right = turned[j] if j < COL_PAD else 0.0
                pieces.append(jnp.where(valid, jnp.where(lane < shift, left, right), 0.0))
            for top in range(0, window, 8 * BATCH):
                spots, sums = [], []
                for row in range(top, min(top + 8 * BATCH, window), 8):
                    at = row + jnp.where(row < split_at + delta, upper_at, lower_at)
                    for j in range(COL_PAD + 1):
                        spot = (col_tile + j, pl.ds(at, 8), slice(None))
                        spots.append(spot)
                        sums.append(canvas[spot] + pieces[j][row : row + 8])
                for spot, value in zip(spots, sums):
                    canvas[spot] = value

    def pair(n, carry):
        slot = 2 * (n & 1)
        start(2 * n + 2, 2 - slot)
        start(2 * n + 3, 3 - slot)
        infos = [place(2 * n), place(2 * n + 1)]
        for half in range(2):
            fetch(2 * n + half, slot + half, lambda copy: copy.wait())
        for half in range(2):
            down_pass(infos[half], slot + half, half)
        for half in range(2):
            across_pass(infos[half], half)
        return carry

    lax.fori_loop(0, count >> 1, pair, 0)

    @pl.when((count & 1) == 1)
    def _():
        last = count - 1
        slot = last & 3
        info = place(last)
        fetch(last, slot, lambda copy: copy.wait())
        down_pass(info, slot, 0)
        across_pass(info, 0)

    if not split:
        stores = canvas_copies(outs[0], True)
        for store in stores:
            store.start()
        for store in stores:
            store.wait()
        return

    for load in late:
        load.wait()
    mixed = slots == 2
    stores = []
    for kind, out in enumerate(outs):
        for i in range(slots):
            slot = row_at ^ (slots - 1 - i)
            side = col_at if kind == 1 else 1 - col_at
            if mixed:
                odd = core == 1
                slot = jnp.where(odd, row_at ^ (1 - kind), slot)
                side = jnp.where(odd, col_at ^ (1 - i), side)
            at = pl.multiple_of(row_pad + slot * stripe, PAD)
            for j in range(TILE_COLS):
                piece = canvas[COL_PAD + side * TILE_COLS + j, pl.ds(at, stripe), :]
                if has_start:
                    from_row = pl.multiple_of(slot * stripe, stripe)
                    piece = piece + early_ref[side * TILE_COLS + j, pl.ds(from_row, stripe), :]
                stages[kind][i, :, j * LANES : (j + 1) * LANES] = piece.astype(out.dtype)
            for n in range(STREAMS):
                size = stripe // STREAMS
                store = pltpu.make_async_copy(
                    stages[kind].at[i, pl.ds(n * size, size)],
                    out.at[pl.ds(i * stripe + n * size, size)],
                    side_sems.at[10 + (kind * slots + i) * STREAMS + n],
                )
                store.start()
                stores.append(store)
    for store in stores:
        store.wait()


def make_quarter(geom, step, table, images, lists, bands, start=None, split=True, after=(), fields=None):
    stripe, slots = geom
    groups, gap, window, parts, group_rows, row_pad = geometry(stripe)
    rows = slots * stripe
    smem = pl.BlockSpec(memory_space=pltpu.SMEM)
    hbm = pl.BlockSpec(memory_space=pl.ANY)
    sources = len(images)
    has_start = start is not None
    extra = 0 if fields is None else FIELD_ROWS
    if split:
        out_shape = [
            jax.ShapeDtypeStruct((rows + extra, SIDE), jnp.bfloat16),
            jax.ShapeDtypeStruct((rows, SIDE), jnp.bfloat16),
        ]
    else:
        out_shape = [jax.ShapeDtypeStruct((QUARTER_COLS, rows, LANES), jnp.float32)]
    stages = [pltpu.VMEM((slots, stripe, SIDE), item.dtype) for item in out_shape] if split else []
    token = jax.ShapeDtypeStruct((1, 1), jnp.float32)
    return pl.pallas_call(
        functools.partial(quarter_kernel, geom, step, sources, has_start, split, len(after), fields is not None),
        out_shape=out_shape + [token],
        in_specs=[smem] * (1 + 2 * sources)
        + [hbm] * sources
        + [hbm, hbm]
        + ([hbm] if has_start else [])
        + [hbm] * (len(after) + (fields is not None)),
        out_specs=[hbm] * len(out_shape) + [smem],
        scratch_shapes=[
            pltpu.VMEM((COL_TILES, 2 * row_pad + rows, LANES), jnp.float32),
            pltpu.VMEM((4, groups * group_rows, BLOCK), jnp.bfloat16),
            pltpu.VMEM((2 * groups, window, BASES * BLOCK), jnp.bfloat16),
            pltpu.VMEM(bands[0].shape, jnp.bfloat16),
            pltpu.VMEM(bands[1].shape, jnp.bfloat16),
            pltpu.SMEM((sources * images[0].shape[0] + 1,), jnp.int32),
            pltpu.SemaphoreType.DMA((4, 2 * groups)),
            pltpu.SemaphoreType.DMA((10 + STREAMS * 2 * slots,)),
        ]
        + stages
        + ([pltpu.VMEM((QUARTER_COLS, rows, LANES), jnp.float32)] if has_start else []),
        compiler_params=pltpu.CompilerParams(vmem_limit_bytes=63 * 1024 * 1024),
        cost_estimate=pl.CostEstimate(flops=1 << 20, bytes_accessed=1 << 20, transcendentals=0),
    )(table, *lists, *images, *bands, *([start] if has_start else []), *after, *([] if fields is None else [fields]))


def merge(stripe, jobs, after=()):
    halves = 2
    size = stripe // halves
    operands, plan = [], []
    for base, row, addends, known in jobs:
        plan.append((len(operands), row, [start for _, start in addends], known is not None))
        operands += [base] + [value for value, _ in addends] + ([] if known is None else [known])
    count = sum(1 + len(starts) for _, _, starts, _ in plan)

    def kernel(*refs):
        inputs = refs[: len(operands)]
        outs = refs[len(operands) + len(after) :][: len(jobs)]
        token_ref = refs[len(operands) + len(after) + len(jobs)]
        scratch = refs[len(operands) + len(after) + len(jobs) + 1 :]
        wide, narrow, staged, sems, out_sems = scratch
        token_ref[0, 0] = 0.0
        copies, lists, which, where = [], [], 0, 0
        for n, (at, row, starts, has_known) in enumerate(plan):
            sources = [(inputs[at], row, wide.at[n])]
            for m, start in enumerate(starts):
                sources.append((inputs[at + 1 + m], start, narrow.at[where + m]))
            where += len(starts)
            per_half = []
            for h in range(halves):
                group = []
                for m, (ref, start, to) in enumerate(sources):
                    copy = pltpu.make_async_copy(
                        ref.at[pl.ds(start + h * size, size)],
                        to.at[pl.ds(h * size, size)],
                        sems.at[which + m, h],
                    )
                    copy.start()
                    group.append(copy)
                per_half.append(group)
            which += len(sources)
            copies.append(per_half)
            if has_known:
                lists.append(
                    pltpu.make_async_copy(
                        inputs[at + 1 + len(starts)],
                        outs[n].at[pl.ds(stripe, FIELD_ROWS)],
                        out_sems.at[n, halves],
                    )
                )
                lists[-1].start()
        where = 0
        for n, (at, row, starts, has_known) in enumerate(plan):
            for h in range(halves):
                for copy in copies[n][h]:
                    copy.wait()
                rows = pl.ds(h * size, size)
                total = wide[n, rows, :].astype(jnp.float32)
                for m in range(len(starts)):
                    total = total + narrow[where + m, rows, :].astype(jnp.float32)
                staged[n, rows, :] = total.astype(jnp.bfloat16)
                store = pltpu.make_async_copy(
                    staged.at[n, rows], outs[n].at[rows], out_sems.at[n, h]
                )
                store.start()
                lists.append(store)
            where += len(starts)
        for copy in lists:
            copy.wait()

    hbm = pl.BlockSpec(memory_space=pl.ANY)
    shapes = [
        jax.ShapeDtypeStruct((stripe + (FIELD_ROWS if has_known else 0), SIDE), jnp.bfloat16)
        for _, _, _, has_known in plan
    ]
    out = pl.pallas_call(
        kernel,
        out_shape=shapes + [jax.ShapeDtypeStruct((1, 1), jnp.float32)],
        in_specs=[hbm] * (len(operands) + len(after)),
        out_specs=[hbm] * len(shapes) + [pl.BlockSpec(memory_space=pltpu.SMEM)],
        scratch_shapes=[
            pltpu.VMEM((len(jobs), stripe, SIDE), jobs[0][0].dtype),
            pltpu.VMEM((count - len(jobs), stripe, SIDE), jnp.bfloat16),
            pltpu.VMEM((len(jobs), stripe, SIDE), jnp.bfloat16),
            pltpu.SemaphoreType.DMA((count, halves)),
            pltpu.SemaphoreType.DMA((len(jobs), halves + 1)),
        ],
        compiler_params=pltpu.CompilerParams(vmem_limit_bytes=63 * 1024 * 1024),
        cost_estimate=pl.CostEstimate(flops=0, bytes_accessed=0, transcendentals=0),
    )(*operands, *after)
    return out[: len(jobs)], out[-1][0, 0]


def on_device(
    expo_count, patch_count, images, block_weight, block_patch, block_offset, kernel_index, coef_table
):
    stripe = SIDE // expo_count
    slots = expo_count // 2
    depth = patch_count // 2
    mixed = slots == 2
    expo, patch = lax.axis_index("expo"), lax.axis_index("patch")
    everyone = [(e, p) for e in range(expo_count) for p in range(patch_count)]

    def swap(value, partner):
        route = []
        for e, p in everyone:
            to_e, to_p = partner(e, p)
            route.append((e * patch_count + p, to_e * patch_count + to_p))
        return lax.ppermute(value, ("expo", "patch"), route)

    def twin(e, p):
        return e ^ 1, p

    def first_partner(e, p):
        if mixed and e % 2 == 1:
            return e ^ 2, p
        return e, p ^ 1

    twin_images = swap(images, twin)
    weights = block_weight.astype(jnp.float32)
    places = jnp.stack(
        [
            (block_patch[:, 0] // PGX) * SIDE + block_offset[:, 0],
            (block_patch[:, 0] % PGX) * SIDE + block_offset[:, 1],
            kernel_index,
        ]
    )
    own = (places, weights)
    other = (swap(places, twin), swap(weights, twin))
    both = own + other
    table = coef_table.T
    bands = make_bands(stripe)

    def digits(places, weights):
        parts = [places[0] // LANES, places[0] % LANES, places[1] // LANES, places[1] % LANES]
        return jnp.stack([part.astype(jnp.bfloat16) for part in parts] + [weights.astype(jnp.bfloat16)])

    fields = jnp.concatenate([digits(*own), digits(*other)], axis=1)

    def full(known):
        return jnp.pad(known, ((0, FIELD_ROWS - known.shape[0]), (0, SIDE - known.shape[1])))

    def known_in(value, count):
        return value[-FIELD_ROWS:][: fields.shape[0], :count]

    table = coef_table.T
    bands = make_bands(stripe)

    def quarter(step, *args, **kwargs):
        return make_quarter((stripe, slots), step, table, *args, **kwargs)

    def own_job(entry, extra, known=None):
        _, stay, got, received = entry
        row = (slots - 1) * stripe
        addends = [(got, row)] + [(value, 0) for value in received + extra]
        return stay, row, addends, None if known is None else full(known)

    def part_jobs(entry, known=None):
        _, stay, got, _ = entry
        jobs = []
        for hop in range(1, slots):
            row = (slots - 1 - hop) * stripe
            jobs.append((stay, row, [(got, row)], None if known is None else full(known)))
        return jobs

    def second_swap(entry, parts):
        for hop, part in enumerate(parts, 1):

            def partner(e, p, hop=hop):
                if mixed and e % 2 == 1:
                    return e, p ^ 1
                return e ^ (2 * hop), p

            entry[3].append(swap(part, partner))

    carried = {}

    def forward(step, sent):
        low = step & -step
        moved = swap(sent, lambda e, p: (e, p ^ (2 * low)))
        carried.setdefault(step ^ low, []).append(moved)
        return moved

    steps = list(range(depth))[::-1]
    early = quarter(
        steps[0], [images], own, bands, split=False
    )[0]
    leave, stay, _ = quarter(
        steps[0], [twin_images], other, bands, start=early, fields=full(fields)
    )

    known, entries, moved = fields, [], {}

    def add_lists(values):
        return jnp.concatenate([known] + [known_in(v, known.shape[1]) for v in values], axis=1)

    def send_on(done, entry, after, lists_done=None, lists_entry=None):
        jobs = [] if done is None else [own_job(done, carried.get(done[0], []), lists_done)]
        sums, token = merge(stripe, jobs + part_jobs(entry, lists_entry), after)
        if done is not None:
            moved[done[0]] = forward(done[0], sums[0])
        second_swap(entry, sums[len(jobs) :])
        return sums, token

    for n, step in enumerate(steps):
        entries.append([step, stay, swap(leave, first_partner), []])
        after = [leave]
        if n == 1:
            known = add_lists([entries[0][2]])
            after += send_on(None, entries[0], after, None, known)[0]
        elif n > 1:
            done, lists_now = entries[n - 2], None
            if n < 4:
                known = lists_now = add_lists(done[3] if n == 2 else carried[done[0]][:1])
            after += send_on(done, entries[n - 1], after, lists_now)[0]
        if step:
            leave, stay, _ = quarter(step - 1, [images, twin_images], both, bands, after=after)
    done, entry = entries[-2:]
    sums, _ = merge(stripe, [own_job(done, carried.get(done[0], []))])
    moved[done[0]] = forward(done[0], sums[0])
    _, token = send_on(None, entry, sums)
    known = add_lists([moved[depth - 2]]) + token.astype(jnp.bfloat16)
    reach = 8
    while reach < patch_count:
        known = jnp.concatenate([known, swap(known, lambda e, p, r=reach: (e, p ^ r))], axis=1)
        reach *= 2

    base, row, addends, _ = own_job(entries[-1], carried[0])
    result = base[row : row + stripe].astype(jnp.float32)
    for value, start in addends:
        if value is addends[-1][0]:
            result = lax.optimization_barrier(result)
        result = result + value[start : start + stripe].astype(jnp.float32)

    places = known[:4].astype(jnp.int32)
    top = places[0] * LANES + places[1] - MARGIN
    left = places[2] * LANES + places[3] - MARGIN
    my_row = (patch // PGX) * SIDE + expo * stripe + jnp.arange(stripe)
    my_col = (patch % PGX) * SIDE + jnp.arange(SIDE)
    row_gap = my_row[:, None] - top[None, :]
    col_gap = my_col[None, :] - left[:, None]
    row_in = jnp.where((row_gap >= 0) & (row_gap < BLOCK), known[4][None, :], 0.0)
    col_in = (col_gap >= 0) & (col_gap < BLOCK)
    weight_map = jnp.dot(
        row_in.astype(jnp.bfloat16),
        col_in.astype(jnp.bfloat16),
        preferred_element_type=jnp.float32,
    )

    coadd_map = result / jnp.maximum(weight_map, weight_floor)
    return (coadd_map[None], weight_map[None])


def solution(mesh):
    return jax.shard_map(
        functools.partial(on_device, mesh.shape["expo"], mesh.shape["patch"]),
        mesh=mesh,
        in_specs=(
            P(("expo", "patch"), None, None),
            P(("expo", "patch")),
            P(("expo", "patch"), None),
            P(("expo", "patch"), None),
            P(("expo", "patch")),
            P(),
        ),
        out_specs=(P("patch", "expo", None), P("patch", "expo", None)),
        check_vma=False,
    )
```

```python
import functools

import jax
import jax.numpy as jnp
import ml_dtypes
import numpy as np
from jax import lax
from jax.experimental import pallas as pl
from jax.experimental.pallas import tpu as pltpu
from jax.sharding import PartitionSpec as P

BLOCK = 512
KHALF = 10
BASES = 3
SIDE = 1024
MARGIN = 128
PGX = 4
PGX_BITS = 2
SIGMAS = (0.8, 1.6, 3.2)
weight_floor = 0.5

LANES = 128
HALF = BLOCK // 2
PAD = 16
BATCH = 4
STREAMS = 2
NEW_META = True
FIELD_ROWS = 16
COL_PAD = BLOCK // LANES
TILE_COLS = SIDE // LANES
QUARTER_COLS = 2 * TILE_COLS
COL_TILES = QUARTER_COLS + 2 * COL_PAD


def taps_at(basis, distance):
    offsets = np.arange(-KHALF, KHALF + 1).astype(np.float32)
    taps = []
    for sigma in SIGMAS:
        profile = np.exp(-offsets * offsets / np.float32(2.0 * sigma * sigma))
        taps.append(profile / np.sum(profile, dtype=np.float32))
    taps = np.stack(taps).astype(ml_dtypes.bfloat16)
    inside = np.abs(distance) <= KHALF
    found = taps[basis, np.where(inside, distance + KHALF, 0)]
    return np.where(inside, found, np.zeros((), ml_dtypes.bfloat16))


def geometry(stripe):
    groups = HALF // stripe
    gap = PAD if groups == 1 else 2 * PAD
    window = stripe + PAD + gap
    parts = 2 if groups == 1 else 1
    group_rows = PAD + 2 * stripe + gap + stripe + 2 * PAD
    row_pad = HALF + PAD + gap
    return groups, gap, window, parts, group_rows, row_pad


def make_bands(stripe):
    _, _, window, parts, _, _ = geometry(stripe)
    height = window // parts
    row, col = np.indices((BASES * height, height + 2 * PAD))
    down = taps_at(row // height, col - row % height - PAD)
    row, col = np.indices((2 * LANES, 2 * LANES))
    across = []
    for side, (low, high) in enumerate(((0, 192), (192, 320), (320, BLOCK))):
        mine = (col + side * LANES >= low) & (col + side * LANES < high)
        for b in range(BASES):
            across.append(np.where(mine, taps_at(np.full_like(row, b), col - row), 0))
    across = np.concatenate(across, axis=0)
    return jnp.asarray(down, jnp.bfloat16), jnp.asarray(across, jnp.bfloat16)


def quarter_kernel(geom, step, sources, has_start, split, waits, has_fields, *refs):
    stripe, slots = geom
    groups, gap, window, parts, group_rows, row_pad = geometry(stripe)
    height = window // parts
    refs = list(refs)
    table_ref = refs.pop(0)
    lists = [(refs.pop(0), refs.pop(0)) for _ in range(sources)]
    images = [refs.pop(0) for _ in range(sources)]
    band_hbm = [refs.pop(0), refs.pop(0)]
    start_ref = refs.pop(0) if has_start else None
    refs = refs[waits:]
    fields_ref = refs.pop(0) if has_fields else None
    outs = [refs.pop(0) for _ in range(2 if split else 1)]
    token_ref = refs.pop(0)
    canvas, tile_buf, spread, down_ref, band_ref, chosen, sems, side_sems = refs[:8]
    stages = refs[8:10]
    early_ref = refs[10] if has_start else None
    expo, place_at = lax.axis_index("expo"), lax.axis_index("patch")
    core, row_at, col_at, quarter = expo & 1, expo >> 1, place_at & 1, (place_at >> 1) ^ step
    rows = slots * stripe
    per_source = images[0].shape[0]

    def canvas_copies(other, out):
        copies = []
        for n in range(4):
            cols = pl.ds(n * (QUARTER_COLS // 4), QUARTER_COLS // 4)
            far = other.at[cols]
            if out:
                copies.append(pltpu.make_async_copy(stages[0].at[cols], far, side_sems.at[2 + n]))
            else:
                copies.append(pltpu.make_async_copy(far, early_ref.at[cols], side_sems.at[2 + n]))
        return copies

    late = []
    third = band_ref.shape[0] // 3
    loads = [pltpu.make_async_copy(band_hbm[0], down_ref, side_sems.at[0])]
    for n in range(3):
        part = pl.ds(n * third, third)
        loads.append(
            pltpu.make_async_copy(band_hbm[1].at[part], band_ref.at[part], side_sems.at[7 + n])
        )
    if has_start:
        late = canvas_copies(start_ref, False)
    if has_fields:
        loads.append(
            pltpu.make_async_copy(
                fields_ref, outs[0].at[pl.ds(rows, FIELD_ROWS)], side_sems.at[6]
            )
        )
    token_ref[0, 0] = 0.0
    for load in loads:
        load.start()

    stripe_bits = stripe.bit_length() - 1
    row_shift = BLOCK - MARGIN - (quarter >> 1) * SIDE
    col_shift = BLOCK - MARGIN - (quarter & 1) * (2 * SIDE)

    def located(top, left):
        row, col = top + row_shift, left + col_shift
        return (row >> stripe_bits) - BLOCK // stripe, row & (stripe - 1), col

    def look_up(k, pick):
        value = pick(lists[0], jnp.minimum(k, per_source - 1))
        for n in range(1, sources):
            other = pick(lists[n], jnp.maximum(k - n * per_source, 0))
            value = jnp.where(k < n * per_source, value, other)
        return value

    def entry(k, field):
        return look_up(k, lambda item, i: item[0][field, i])

    count = jnp.int32(0)
    for n, (place_ref, _) in enumerate(lists):

        def scan(i, count, n=n, place_ref=place_ref):
            stripe_at, rho, col = located(place_ref[0, i], place_ref[1, i])
            lowest = jnp.maximum(stripe_at, 0)
            lowest = lowest + ((lowest + core) & 1)
            highest = stripe_at + BLOCK // stripe - (rho == 0).astype(jnp.int32)
            hit = (lowest <= jnp.minimum(highest, 2 * slots - 1)) & (col > 0)
            hit = hit & (col < BLOCK + 2 * SIDE)
            chosen[count] = i + n * per_source
            return count + hit.astype(jnp.int32)

        count = lax.fori_loop(0, per_source, scan, count)

    def pieces_of(g):
        top, base = 2 * stripe * g, group_rows * g
        early = PAD if g > 0 else 0
        late = PAD if g < groups - 1 else 0
        again = base + PAD + 2 * stripe + gap
        return [
            (top - early, early + 2 * stripe + late, base + PAD - early),
            (top - early, early + stripe + PAD, again - early),
        ]

    def fetch(i, slot, act):
        k = chosen[i]
        for n, image_ref in enumerate(images):

            @pl.when((k >= n * per_source) & (k < (n + 1) * per_source))
            def _():
                for g in range(groups):
                    for c, (top, size, to) in enumerate(pieces_of(g)):
                        act(
                            pltpu.make_async_copy(
                                image_ref.at[k - n * per_source, pl.ds(top, size), :],
                                tile_buf.at[slot, pl.ds(to, size), :],
                                sems.at[slot, 2 * g + c],
                            )
                        )

    def start(i, slot):
        @pl.when(i < count)
        def _():
            fetch(i, slot, lambda copy: copy.start())

    for slot in range(4):
        for g in range(groups):
            base = group_rows * g
            again = base + PAD + 2 * stripe + gap
            for top, bottom in (
                (base, base + PAD),
                (base + PAD + 2 * stripe, again),
                (again + stripe + PAD, base + group_rows),
            ):
                tile_buf[slot, top:bottom, :] = jnp.zeros((bottom - top, BLOCK), tile_buf.dtype)
    start(0, 0)
    start(1, 1)
    for load in late:
        load.start()
    canvas[COL_PAD : COL_PAD + QUARTER_COLS, row_pad : row_pad + rows, :] = jnp.zeros(
        (QUARTER_COLS, rows, LANES), jnp.float32
    )
    for load in loads:
        load.wait()

    def place(i):
        k = chosen[i]
        stripe_at, rho, col = located(entry(k, 0), entry(k, 1))
        col_tile = col >> 7
        shift = col & (LANES - 1)
        parted = ((stripe_at + core) & 1) == 0
        slot_row = stripe * ((stripe_at + 1 - core) >> 1)
        first = jnp.where(parted, 2 * stripe - rho, stripe - rho)
        first_at = pl.multiple_of((first >> 4) << 4, PAD)
        delta = first - first_at
        return k, rho, col_tile, shift, parted, slot_row, first_at, delta

    def down_pass(info, slot, half):
        k, first_at = info[0], info[6]
        kernel = entry(k, 2)
        weight = look_up(k, lambda item, i: item[1][i])
        scales = [table_ref[b, kernel] * weight for b in range(BASES)]
        for g in range(groups):
            for part in range(parts):
                at = pl.multiple_of(g * group_rows + first_at + part * height, PAD)
                result = jnp.dot(
                    down_ref[...],
                    tile_buf[slot, pl.ds(at, height + 2 * PAD), :],
                    preferred_element_type=jnp.float32,
                )
                for b in range(BASES):
                    spread[
                        half * groups + g,
                        part * height : (part + 1) * height,
                        b * BLOCK : (b + 1) * BLOCK,
                    ] = (result[b * height : (b + 1) * height] * scales[b]).astype(jnp.bfloat16)

    def across_pass(info, half):
        k, rho, col_tile, shift, parted, slot_row, first_at, delta = info
        lane = lax.broadcasted_iota(jnp.int32, (window, LANES), 1)
        local = lax.broadcasted_iota(jnp.int32, (window, LANES), 0) - delta
        split_at = jnp.where(parted, rho, stripe)
        last = jnp.where(parted, stripe + gap, stripe)
        valid = (local >= 0) & (
            (local < split_at) | ((local >= rho + gap) & (local < last))
        )
        for g in range(groups):
            wide = []
            for side in range(3):
                acc = None
                for b in range(BASES):
                    lo = b * BLOCK + LANES * side
                    at = (side * BASES + b) * 2 * LANES
                    term = jnp.dot(
                        spread[half * groups + g, :, lo : lo + 2 * LANES],
                        band_ref[at : at + 2 * LANES],
                        preferred_element_type=jnp.float32,
                    )
                    acc = term if acc is None else acc + term
                wide.append(acc)
            merged = jnp.concatenate(
                [
                    wide[0][:, :LANES],
                    wide[0][:, LANES:] + wide[1][:, :LANES],
                    wide[1][:, LANES:] + wide[2][:, :LANES],
                    wide[2][:, LANES:],
                ],
                axis=1,
            )
            turned = [
                pltpu.roll(merged[:, j * LANES : (j + 1) * LANES], shift, 1)
                for j in range(COL_PAD)
            ]
            base = row_pad + slot_row + g * stripe - delta
            upper_at = jnp.where(parted, base + stripe, base)
            lower_at = jnp.where(parted, base - gap, base)
            pieces = []
            for j in range(COL_PAD + 1):
                left = turned[j - 1] if j > 0 else 0.0
                right = turned[j] if j < COL_PAD else 0.0
                pieces.append(jnp.where(valid, jnp.where(lane < shift, left, right), 0.0))
            for top in range(0, window, 8 * BATCH):
                spots, sums = [], []
                for row in range(top, min(top + 8 * BATCH, window), 8):
                    at = row + jnp.where(row < split_at + delta, upper_at, lower_at)
                    for j in range(COL_PAD + 1):
                        spot = (col_tile + j, pl.ds(at, 8), slice(None))
                        spots.append(spot)
                        sums.append(canvas[spot] + pieces[j][row : row + 8])
                for spot, value in zip(spots, sums):
                    canvas[spot] = value

    def pair(n, carry):
        slot = 2 * (n & 1)
        start(2 * n + 2, 2 - slot)
        start(2 * n + 3, 3 - slot)
        infos = [place(2 * n), place(2 * n + 1)]
        for half in range(2):
            fetch(2 * n + half, slot + half, lambda copy: copy.wait())
        for half in range(2):
            down_pass(infos[half], slot + half, half)
        for half in range(2):
            across_pass(infos[half], half)
        return carry

    lax.fori_loop(0, count >> 1, pair, 0)

    @pl.when((count & 1) == 1)
    def _():
        last = count - 1
        slot = last & 3
        info = place(last)
        fetch(last, slot, lambda copy: copy.wait())
        down_pass(info, slot, 0)
        across_pass(info, 0)

    if not split:
        stores = canvas_copies(outs[0], True)
        for n, store in enumerate(stores):
            low, size = n * (QUARTER_COLS // 4), QUARTER_COLS // 4
            piece = canvas[COL_PAD + low : COL_PAD + low + size, row_pad : row_pad + rows, :]
            stages[0][low : low + size] = piece.astype(jnp.bfloat16)
            store.start()
        for store in stores:
            store.wait()
        return

    for load in late:
        load.wait()
    mixed = slots == 2
    stores = []
    for kind, out in enumerate(outs):
        for i in range(slots):
            slot = row_at ^ (slots - 1 - i)
            side = col_at if kind == 1 else 1 - col_at
            if mixed:
                odd = core == 1
                slot = jnp.where(odd, row_at ^ (1 - kind), slot)
                side = jnp.where(odd, col_at ^ (1 - i), side)
            at = pl.multiple_of(row_pad + slot * stripe, PAD)
            for j in range(TILE_COLS):
                piece = canvas[COL_PAD + side * TILE_COLS + j, pl.ds(at, stripe), :]
                if has_start:
                    from_row = pl.multiple_of(slot * stripe, stripe)
                    early = early_ref[side * TILE_COLS + j, pl.ds(from_row, stripe), :]
                    piece = piece + early.astype(jnp.float32)
                stages[kind][i, :, j * LANES : (j + 1) * LANES] = piece.astype(out.dtype)
            for n in range(STREAMS):
                size = stripe // STREAMS
                store = pltpu.make_async_copy(
                    stages[kind].at[i, pl.ds(n * size, size)],
                    out.at[pl.ds(i * stripe + n * size, size)],
                    side_sems.at[10 + (kind * slots + i) * STREAMS + n],
                )
                store.start()
                stores.append(store)
    for store in stores:
        store.wait()


def make_quarter(geom, step, table, images, lists, bands, start=None, split=True, after=(), fields=None):
    stripe, slots = geom
    groups, gap, window, parts, group_rows, row_pad = geometry(stripe)
    rows = slots * stripe
    smem = pl.BlockSpec(memory_space=pltpu.SMEM)
    hbm = pl.BlockSpec(memory_space=pl.ANY)
    sources = len(images)
    has_start = start is not None
    extra = 0 if fields is None else FIELD_ROWS
    if split:
        out_shape = [
            jax.ShapeDtypeStruct((rows + extra, SIDE), jnp.bfloat16),
            jax.ShapeDtypeStruct((rows, SIDE), jnp.bfloat16),
        ]
    else:
        out_shape = [jax.ShapeDtypeStruct((QUARTER_COLS, rows, LANES), jnp.bfloat16)]
    stages = [pltpu.VMEM((slots, stripe, SIDE) if split else item.shape, item.dtype) for item in out_shape]
    token = jax.ShapeDtypeStruct((1, 1), jnp.float32)
    return pl.pallas_call(
        functools.partial(quarter_kernel, geom, step, sources, has_start, split, len(after), fields is not None),
        out_shape=out_shape + [token],
        in_specs=[smem] * (1 + 2 * sources)
        + [hbm] * sources
        + [hbm, hbm]
        + ([hbm] if has_start else [])
        + [hbm] * (len(after) + (fields is not None)),
        out_specs=[hbm] * len(out_shape) + [smem],
        scratch_shapes=[
            pltpu.VMEM((COL_TILES, 2 * row_pad + rows, LANES), jnp.float32),
            pltpu.VMEM((4, groups * group_rows, BLOCK), jnp.bfloat16),
            pltpu.VMEM((2 * groups, window, BASES * BLOCK), jnp.bfloat16),
            pltpu.VMEM(bands[0].shape, jnp.bfloat16),
            pltpu.VMEM(bands[1].shape, jnp.bfloat16),
            pltpu.SMEM((sources * images[0].shape[0] + 1,), jnp.int32),
            pltpu.SemaphoreType.DMA((4, 2 * groups)),
            pltpu.SemaphoreType.DMA((10 + STREAMS * 2 * slots,)),
        ]
        + stages
        + ([pltpu.VMEM((QUARTER_COLS, rows, LANES), jnp.bfloat16)] if has_start else []),
        compiler_params=pltpu.CompilerParams(vmem_limit_bytes=63 * 1024 * 1024),
        cost_estimate=pl.CostEstimate(flops=1 << 20, bytes_accessed=1 << 20, transcendentals=0),
    )(table, *lists, *images, *bands, *([start] if has_start else []), *after, *([] if fields is None else [fields]))


def merge(stripe, jobs, after=()):
    halves = 2
    size = stripe // halves
    operands, plan = [], []
    for base, row, addends, known in jobs:
        plan.append((len(operands), row, [start for _, start in addends], known is not None))
        operands += [base] + [value for value, _ in addends] + ([] if known is None else [known])
    count = sum(1 + len(starts) for _, _, starts, _ in plan)

    def kernel(*refs):
        inputs = refs[: len(operands)]
        outs = refs[len(operands) + len(after) :][: len(jobs)]
        token_ref = refs[len(operands) + len(after) + len(jobs)]
        scratch = refs[len(operands) + len(after) + len(jobs) + 1 :]
        wide, narrow, staged, sems, out_sems = scratch
        token_ref[0, 0] = 0.0
        copies, lists, which, where = [], [], 0, 0
        for n, (at, row, starts, has_known) in enumerate(plan):
            sources = [(inputs[at], row, wide.at[n])]
            for m, start in enumerate(starts):
                sources.append((inputs[at + 1 + m], start, narrow.at[where + m]))
            where += len(starts)
            per_half = []
            for h in range(halves):
                group = []
                for m, (ref, start, to) in enumerate(sources):
                    copy = pltpu.make_async_copy(
                        ref.at[pl.ds(start + h * size, size)],
                        to.at[pl.ds(h * size, size)],
                        sems.at[which + m, h],
                    )
                    copy.start()
                    group.append(copy)
                per_half.append(group)
            which += len(sources)
            copies.append(per_half)
            if has_known:
                lists.append(
                    pltpu.make_async_copy(
                        inputs[at + 1 + len(starts)],
                        outs[n].at[pl.ds(stripe, FIELD_ROWS)],
                        out_sems.at[n, halves],
                    )
                )
                lists[-1].start()
        where = 0
        for n, (at, row, starts, has_known) in enumerate(plan):
            for h in range(halves):
                for copy in copies[n][h]:
                    copy.wait()
                rows = pl.ds(h * size, size)
                total = wide[n, rows, :].astype(jnp.float32)
                for m in range(len(starts)):
                    total = total + narrow[where + m, rows, :].astype(jnp.float32)
                staged[n, rows, :] = total.astype(jnp.bfloat16)
                store = pltpu.make_async_copy(
                    staged.at[n, rows], outs[n].at[rows], out_sems.at[n, h]
                )
                store.start()
                lists.append(store)
            where += len(starts)
        for copy in lists:
            copy.wait()

    hbm = pl.BlockSpec(memory_space=pl.ANY)
    shapes = [
        jax.ShapeDtypeStruct((stripe + (FIELD_ROWS if has_known else 0), SIDE), jnp.bfloat16)
        for _, _, _, has_known in plan
    ]
    out = pl.pallas_call(
        kernel,
        out_shape=shapes + [jax.ShapeDtypeStruct((1, 1), jnp.float32)],
        in_specs=[hbm] * (len(operands) + len(after)),
        out_specs=[hbm] * len(shapes) + [pl.BlockSpec(memory_space=pltpu.SMEM)],
        scratch_shapes=[
            pltpu.VMEM((len(jobs), stripe, SIDE), jobs[0][0].dtype),
            pltpu.VMEM((count - len(jobs), stripe, SIDE), jnp.bfloat16),
            pltpu.VMEM((len(jobs), stripe, SIDE), jnp.bfloat16),
            pltpu.SemaphoreType.DMA((count, halves)),
            pltpu.SemaphoreType.DMA((len(jobs), halves + 1)),
        ],
        compiler_params=pltpu.CompilerParams(vmem_limit_bytes=63 * 1024 * 1024),
        cost_estimate=pl.CostEstimate(flops=0, bytes_accessed=0, transcendentals=0),
    )(*operands, *after)
    return out[: len(jobs)], out[-1][0, 0]


def on_device(
    expo_count, patch_count, images, block_weight, block_patch, block_offset, kernel_index, coef_table
):
    stripe = SIDE // expo_count
    slots = expo_count // 2
    depth = patch_count // 2
    mixed = slots == 2
    expo, patch = lax.axis_index("expo"), lax.axis_index("patch")
    everyone = [(e, p) for e in range(expo_count) for p in range(patch_count)]

    def swap(value, partner):
        route = []
        for e, p in everyone:
            to_e, to_p = partner(e, p)
            route.append((e * patch_count + p, to_e * patch_count + to_p))
        return lax.ppermute(value, ("expo", "patch"), route)

    def twin(e, p):
        return e ^ 1, p

    def first_partner(e, p):
        if mixed and e % 2 == 1:
            return e ^ 2, p
        return e, p ^ 1

    twin_images = swap(images, twin)
    weights = block_weight.astype(jnp.float32)
    places = jnp.stack(
        [
            (block_patch[:, 0] // PGX) * SIDE + block_offset[:, 0],
            (block_patch[:, 0] % PGX) * SIDE + block_offset[:, 1],
            kernel_index,
        ]
    )
    own = (places, weights)
    other = (swap(places, twin), swap(weights, twin))
    both = own + other
    table = coef_table.T
    bands = make_bands(stripe)

    def digits(places, weights):
        parts = [places[0] // LANES, places[0] % LANES, places[1] // LANES, places[1] % LANES]
        return jnp.stack([part.astype(jnp.bfloat16) for part in parts] + [weights.astype(jnp.bfloat16)])

    fields = jnp.concatenate([digits(*own), digits(*other)], axis=1)

    def full(known):
        return jnp.pad(known, ((0, FIELD_ROWS - known.shape[0]), (0, SIDE - known.shape[1])))

    def known_in(value, count):
        return value[-FIELD_ROWS:][: fields.shape[0], :count]

    table = coef_table.T
    bands = make_bands(stripe)

    def quarter(step, *args, **kwargs):
        return make_quarter((stripe, slots), step, table, *args, **kwargs)

    def own_job(entry, extra, known=None):
        _, stay, got, received = entry
        row = (slots - 1) * stripe
        addends = [(got, row)] + [(value, 0) for value in received + extra]
        return stay, row, addends, None if known is None else full(known)

    def part_jobs(entry, known=None):
        _, stay, got, _ = entry
        jobs = []
        for hop in range(1, slots):
            row = (slots - 1 - hop) * stripe
            jobs.append((stay, row, [(got, row)], None if known is None else full(known)))
        return jobs

    def second_swap(entry, parts):
        for hop, part in enumerate(parts, 1):

            def partner(e, p, hop=hop):
                if mixed and e % 2 == 1:
                    return e, p ^ 1
                return e ^ (2 * hop), p

            entry[3].append(swap(part, partner))

    carried = {}

    def forward(step, sent):
        low = step & -step
        moved = swap(sent, lambda e, p: (e, p ^ (2 * low)))
        carried.setdefault(step ^ low, []).append(moved)
        return moved

    steps = list(range(depth))[::-1]
    early = quarter(
        steps[0], [images], own, bands, split=False
    )[0]
    leave, stay, _ = quarter(
        steps[0], [twin_images], other, bands, start=early, fields=full(fields)
    )

    known, entries, moved = fields, [], {}

    def add_lists(values):
        return jnp.concatenate([known] + [known_in(v, known.shape[1]) for v in values], axis=1)

    def send_on(done, entry, after, lists_done=None, lists_entry=None):
        jobs = [] if done is None else [own_job(done, carried.get(done[0], []), lists_done)]
        sums, token = merge(stripe, jobs + part_jobs(entry, lists_entry), after)
        if done is not None:
            moved[done[0]] = forward(done[0], sums[0])
        second_swap(entry, sums[len(jobs) :])
        return sums, token

    for n, step in enumerate(steps):
        entries.append([step, stay, swap(leave, first_partner), []])
        after = [leave]
        if n == 1:
            known = add_lists([entries[0][2]])
            after += send_on(None, entries[0], after, None, known)[0]
        elif n > 1:
            done, lists_now = entries[n - 2], None
            if n < 4:
                known = lists_now = add_lists(done[3] if n == 2 else carried[done[0]][:1])
            after += send_on(done, entries[n - 1], after, lists_now)[0]
        if step:
            leave, stay, _ = quarter(step - 1, [images, twin_images], both, bands, after=after)
    done, entry = entries[-2:]
    sums, _ = merge(stripe, [own_job(done, carried.get(done[0], []))])
    moved[done[0]] = forward(done[0], sums[0])
    _, token = send_on(None, entry, sums)
    known = add_lists([moved[depth - 2]]) + token.astype(jnp.bfloat16)
    reach = 8
    while reach < patch_count:
        known = jnp.concatenate([known, swap(known, lambda e, p, r=reach: (e, p ^ r))], axis=1)
        reach *= 2

    base, row, addends, _ = own_job(entries[-1], carried[0])
    result = base[row : row + stripe].astype(jnp.float32)
    for value, start in addends:
        if value is addends[-1][0]:
            result = lax.optimization_barrier(result)
        result = result + value[start : start + stripe].astype(jnp.float32)

    places = known[:4].astype(jnp.int32)
    top = places[0] * LANES + places[1] - MARGIN
    left = places[2] * LANES + places[3] - MARGIN
    my_row = (patch // PGX) * SIDE + expo * stripe + jnp.arange(stripe)
    my_col = (patch % PGX) * SIDE + jnp.arange(SIDE)
    row_gap = my_row[:, None] - top[None, :]
    col_gap = my_col[None, :] - left[:, None]
    row_in = jnp.where((row_gap >= 0) & (row_gap < BLOCK), known[4][None, :], 0.0)
    col_in = (col_gap >= 0) & (col_gap < BLOCK)
    weight_map = jnp.dot(
        row_in.astype(jnp.bfloat16),
        col_in.astype(jnp.bfloat16),
        preferred_element_type=jnp.float32,
    )

    coadd_map = result / jnp.maximum(weight_map, weight_floor)
    return (coadd_map[None], weight_map[None])


def solution(mesh):
    return jax.shard_map(
        functools.partial(on_device, mesh.shape["expo"], mesh.shape["patch"]),
        mesh=mesh,
        in_specs=(
            P(("expo", "patch"), None, None),
            P(("expo", "patch")),
            P(("expo", "patch"), None),
            P(("expo", "patch"), None),
            P(("expo", "patch")),
            P(),
        ),
        out_specs=(P("patch", "expo", None), P("patch", "expo", None)),
        check_vma=False,
    )
```
